512 devices in a mesh: probe: 16 (over y_hi, x, core), gx: 32 (over z, y_lo).
Axes of the slice: x: 4, y: 4 (y_hi: 2, y_lo: 2; y = y_hi * 2 + y_lo), z: 16, core: 2. Of those that a mesh axis runs over, the one named last changes fastest.
Arguments:
- wavefields: float32 [16, 2, 2, 768, 32, 128], P('probe', None, None, 'gx'), may hold values from -6 to 6
- stiffness: float32 [768, 32, 128], P('gx'), may hold values from 0.05 to 0.2
- buoyancy: float32 [768, 32, 128], P('gx'), may hold values from 0.5 to 1.5
- pert_stiffness: float32 [15, 8, 8, 8], replicated, may hold values from -0.3 to 0.3
- pert_buoyancy: float32 [15, 8, 8, 8], replicated, may hold values from -1.5 to 1.5
- xblock_index: int32 [15], replicated, may hold values from 0 to 95
- zblock_index: int32 [15], replicated, may hold values from 0 to 3
- yblock_index: int32 [15], replicated, may hold values from 0 to 15
- source_xcell: int32 [2], replicated, may hold values from 0 to 767
- source_zcell: int32 [2], replicated, may hold values from 0 to 31
- source_ycell: int32 [2], replicated, may hold values from 0 to 127
- wavelet: float32 [2, 2], replicated, may hold values from -4 to 4
Outputs:
- advanced: float32 [16, 2, 2, 768, 32, 128], P('probe', None, None, 'gx')
The draws below stay inside these ranges and needn't reach their ends.
All inputs are finite; a program needn't handle non-finite values.
Results may differ from the reference program's by a relative error of at most 0.0003.
Values sent between devices are 32-bit elements; how exact they have to be, the bound alone decides.
No kernel may reach another device: no remote copies, remote signals or barrier semaphores. Data moves between devices by JAX's collectives and lax.ppermute only.
A program may use at most 64 MiB of HBM per device.

```python
import jax
import jax.numpy as jnp
from jax import lax

NZ = 32
NY = 128
BLK = 8
ITERS = 2
SHOTS = 2
NX = 768
GROUPS = 16
PROBES = 15


def place_ends(entries, own_key, least, high):
    index_at = [jax.random.randint(jax.random.fold_in(own_key, axis), (), 0, length) for axis, length in enumerate(entries.shape)]
    longest = entries.shape.index(max(entries.shape))
    next_to = index_at[:longest] + [(index_at[longest] + 1) % entries.shape[longest]] + index_at[longest + 1:]
    return entries.at[tuple(index_at)].set(least).at[tuple(next_to)].set(high)


def block_scale(own_key, extent, pieces, low, largest):
    def one(axis_at, shards_of):
        draws = jax.random.uniform(jax.random.fold_in(jax.random.fold_in(own_key, 6), axis_at), (shards_of,), jnp.float32, low / len(pieces), largest / len(pieces))
        return jnp.repeat(jnp.exp(draws), extent[axis_at] // shards_of).reshape((-1,) + (1,) * (len(extent) - axis_at - 1))

    level = one(*pieces[0])
    for cut in pieces[1:]:
        level = level * one(*cut)
    return level


def scatter_about(key, shape, scale, bound, pieces=(), kind=jnp.bfloat16):
    factor_of = block_scale(key, shape, pieces, -0.22, 0.18) if pieces else 1.0
    values = jax.random.normal(key, shape, jnp.float32) * scale * factor_of
    return jnp.minimum(jnp.maximum(values, -bound), bound).astype(kind)


def setup_inputs(seed: int = 0) -> dict:
    key_list = jax.random.split(jax.random.key(seed), 13)
    wavefields = scatter_about(key_list[0], (GROUPS, SHOTS, 2, NX, NZ, NY), 1.0, 6.0, ((0, 16), (3, 32)), jnp.float32)
    stiffness = jnp.clip(0.05 + 0.15 * jax.random.uniform(key_list[1], (NX, NZ, NY), jnp.float32) ** block_scale(key_list[1], (NX, NZ, NY), ((0, 32),), -0.2, 0.2), 0.05, 0.2)
    buoyancy = jnp.clip(0.5 + 1.0 * jax.random.uniform(key_list[2], (NX, NZ, NY), jnp.float32) ** block_scale(key_list[2], (NX, NZ, NY), ((0, 32),), -0.2, 0.2), 0.5, 1.5)
    pert_stiffness = scatter_about(key_list[3], (PROBES, BLK, BLK, BLK), 0.05, 0.3, (), jnp.float32)
    pert_buoyancy = scatter_about(key_list[4], (PROBES, BLK, BLK, BLK), 0.3, 1.5, (), jnp.float32)
    xblock_index = place_ends(jax.random.randint(key_list[5], (PROBES,), 0, NX // BLK), jax.random.fold_in(key_list[5], 1), 0, (NX // BLK) - 1).astype(jnp.int32)
    zblock_index = place_ends(jax.random.randint(key_list[6], (PROBES,), 0, NZ // BLK), jax.random.fold_in(key_list[6], 1), 0, (NZ // BLK) - 1).astype(jnp.int32)
    yblock_index = place_ends(jax.random.randint(key_list[7], (PROBES,), 0, NY // BLK), jax.random.fold_in(key_list[7], 1), 0, (NY // BLK) - 1).astype(jnp.int32)
    source_xcell = jax.random.randint(key_list[8], (SHOTS,), 0, NX).astype(jnp.int32)
    source_zcell = jax.random.randint(key_list[9], (SHOTS,), 0, NZ).astype(jnp.int32)
    source_ycell = jax.random.randint(key_list[10], (SHOTS,), 0, NY).astype(jnp.int32)
    wavelet = scatter_about(key_list[11], (SHOTS, ITERS), 1.0, 4.0, (), jnp.float32)
    return dict(wavefields=wavefields, stiffness=stiffness, buoyancy=buoyancy, pert_stiffness=pert_stiffness, pert_buoyancy=pert_buoyancy, xblock_index=xblock_index, zblock_index=zblock_index, yblock_index=yblock_index, source_xcell=source_xcell, source_zcell=source_zcell, source_ycell=source_ycell, wavelet=wavelet)


def shifted(values, dimension, offset):
    selector = [slice(None)] * values.ndim
    for inner in range(values.ndim - 3, values.ndim):
        selector[inner] = slice(1, values.shape[inner] - 1)
    selector[dimension] = slice(1 + offset, values.shape[dimension] - 1 + offset)
    return values[tuple(selector)]


def stencil(padded, coefficient):
    centre = shifted(padded, padded.ndim - 1, 0)
    centre_c = shifted(coefficient, coefficient.ndim - 1, 0)
    summed = None
    for which in range(3):
        for offset in (1, -1):
            neighbour = shifted(padded, padded.ndim - 3 + which, offset)
            neighbour_c = shifted(coefficient, coefficient.ndim - 3 + which, offset)
            termed = 0.5 * (centre_c + neighbour_c) * (neighbour - centre)
            summed = termed if summed is None else summed + termed
    return summed


def padall(values):
    return jnp.pad(values, [(0, 0)] * (values.ndim - 3) + [(1, 1)] * 3)


def place(values, xstart, zstart, ystart):
    zeros = jnp.zeros((NX, NZ, NY), jnp.float32)
    starts = (xstart.astype(jnp.int32) * BLK, zstart.astype(jnp.int32) * BLK, ystart.astype(jnp.int32) * BLK)
    return lax.dynamic_update_slice(zeros, values.astype(jnp.float32), starts)


def reference(wavefields, stiffness, buoyancy, pert_stiffness, pert_buoyancy, xblock_index, zblock_index, yblock_index, source_xcell, source_zcell, source_ycell, wavelet):
    earlier = wavefields[:, :, 0]
    present = wavefields[:, :, 1]
    stiff_block = jax.vmap(place)(pert_stiffness, xblock_index, zblock_index, yblock_index)
    buoy_block = jax.vmap(place)(pert_buoyancy, xblock_index, zblock_index, yblock_index)
    buoy_padded = padall(buoyancy)
    block_padded = padall(buoy_block)[:, None]
    shot_rows = jnp.arange(SHOTS, dtype=jnp.int32)
    for instant in range(ITERS):
        laplace = stencil(padall(present), buoy_padded)
        born_term = stiff_block[:, None] * laplace[0][None] + stiffness * stencil(padall(present[0])[None], block_padded)
        injected = jnp.zeros((SHOTS, NX, NZ, NY), jnp.float32).at[shot_rows, source_xcell, source_zcell, source_ycell].add(wavelet[:, instant])
        forcing = jnp.concatenate([injected[None], born_term], 0)
        upcoming = 2.0 * present - earlier + stiffness * laplace + forcing
        earlier, present = present, upcoming
    return jnp.stack([earlier, present], 2)
```

```python
import functools

import jax
import jax.numpy as jnp
from jax import lax
from jax.experimental import pallas as pl
from jax.experimental.pallas import tpu as pltpu
from jax.sharding import PartitionSpec as P

EDGE = 8
SPAN = EDGE + 4
PER_ROW = 10
STRIPS = [(s, 1, i) for s in range(2) for i in range(SPAN)] + [
    (s, 0, i) for s in range(2) for i in range(1, SPAN - 1)
]
PIECE = (64, 128)

FIRST = (1, 2, 6)
NEXT = ((9, 3, 7, 5), (10, 4, 12), (14, 15))
DIRECT = (8, 11, 13)

ANY = pl.BlockSpec(memory_space=pl.ANY)
SMEM = pl.BlockSpec(memory_space=pltpu.SMEM)
PARAMS = pltpu.CompilerParams(vmem_limit_bytes=32 * 1024 * 1024)


def copy_all(pairs, sems):
    copies = [pltpu.make_async_copy(a, b, sems.at[n]) for n, (a, b) in enumerate(pairs)]
    for copy in copies:
        copy.start()
    return copies


def wait_all(copies):
    for copy in copies:
        copy.wait()


def wrapped(shift):
    return jnp.bitwise_and(shift + 128, 127)


def split_kernel(
    width, xb, zb, yb, wave, stiff, buoy, low, high, p0, p1, p2, d0, d1, d2, slab, packed, sem, sem_slab, sem_out
):
    first = lax.axis_index("gx") * width
    edges = []
    for out, outer, inner in ((low, 0, 0), (high, width - 1, width - 2)):
        for s in range(2):
            edges.append((wave.at[s, 1, pl.ds(inner, 2)], out.at[pl.ds(2 * s, 2)]))
            edges.append((wave.at[s, 0, outer], out.at[4 + s]))
        edges.append((buoy.at[pl.ds(inner, 2)], out.at[pl.ds(6, 2)]))
        edges.append((stiff.at[outer], out.at[8]))
    edges = copy_all(edges, sem)

    def start_of(g):
        return xb[g] * EDGE - 2 - first

    def touches(g):
        x0 = start_of(g)
        return (x0 < width) & (x0 + SPAN > 0)

    def some(g, found):
        return found | touches(g).astype(jnp.int32)

    needed = lax.fori_loop(0, 15, some, jnp.int32(0))

    @pl.when((lax.axis_index("probe") == 0) & (needed > 0))
    def _():
        load = pltpu.make_async_copy(wave, slab.at[:, :, :, pl.ds(8, 32)], sem_slab)
        load.start()
        load.wait()
        lane = lax.broadcasted_iota(jnp.int32, (16, 128), 1)

        def one(g, at):
            x0 = start_of(g)
            r0 = zb[g] * EDGE + 6
            y0 = yb[g] * EDGE - 2
            for k in range(0, len(STRIPS), PER_ROW):
                row = jnp.zeros((16, 128), jnp.float32)
                for q, (s, t, i) in enumerate(STRIPS[k : k + PER_ROW]):
                    plane = jnp.clip(x0 + i, 0, width - 1)
                    values = slab[s, t, plane, pl.ds(r0, 16), :]
                    values = pltpu.roll(values, wrapped(SPAN * q - y0), 1)
                    row = jnp.where((lane >= SPAN * q) & (lane < SPAN * (q + 1)), values, row)
                packed[at, pl.ds(k // PER_ROW * SPAN, 16), :] = row

        at = 0
        spots = []
        for head, rest in zip(FIRST, NEXT):
            spots += [head, *rest]
        spots += DIRECT
        for at, probe in enumerate(spots):

            @pl.when(touches(probe - 1))
            def _():
                one(probe - 1, at)

        outs, at = [], 0
        for out, rest in zip((p0, p1, p2), NEXT):
            outs.append((packed.at[pl.ds(at, 1 + len(rest))], out))
            at += 1 + len(rest)
        for out in (d0, d1, d2):
            outs.append((packed.at[at], out))
            at += 1
        wait_all(copy_all(outs, sem_out))

    wait_all(edges)


def pass_kernel(r0, r1, r2, q0, q1, q2, q3, sem):
    row = lax.axis_index("probe")
    for head, rest, got in zip(FIRST, NEXT, (r0, r1, r2)):

        @pl.when(row == head)
        def _():
            pairs = [(got.at[1 + n], out) for n, out in zip(range(len(rest)), (q0, q1, q2, q3))]
            wait_all(copy_all(pairs, sem))


def pick_kernel(r0, r1, r2, d0, d1, d2, q0, q1, q2, q3, out, sem):
    row = lax.axis_index("probe")

    def bring(where, source):
        @pl.when(where)
        def _():
            copy = pltpu.make_async_copy(source, out, sem)
            copy.start()
            copy.wait()

    for head, got in zip(FIRST, (r0, r1, r2)):
        bring(row == head, got.at[0])
    for target, got in zip(DIRECT, (d0, d1, d2)):
        bring(row == target, got)
    for n, got in enumerate((q0, q1, q2, q3)):
        where = row < 0
        for rest in NEXT:
            if n < len(rest):
                where = where | (row == rest[n])
        bring(where, got)


def march_kernel(
    width, sx, sz, sy, wavelet, wave, stiff, buoy, below, above, out, pres, prev, cext, kext, mid, o1, o2, sem, sem_out
):
    rows = pl.ds(8, 32)
    loads = []
    for s in range(2):
        loads.append((wave.at[s, 1], pres.at[s, pl.ds(2, width), rows]))
        loads.append((below.at[pl.ds(2 * s, 2)], pres.at[s, pl.ds(0, 2), rows]))
        loads.append((above.at[pl.ds(2 * s, 2)], pres.at[s, pl.ds(width + 2, 2), rows]))
        loads.append((wave.at[s, 0], prev.at[s, pl.ds(1, width)]))
        loads.append((below.at[4 + s], prev.at[s, 0]))
        loads.append((above.at[4 + s], prev.at[s, width + 1]))
    loads.append((buoy, cext.at[pl.ds(2, width), rows]))
    loads.append((below.at[pl.ds(6, 2)], cext.at[pl.ds(0, 2), rows]))
    loads.append((above.at[pl.ds(6, 2)], cext.at[pl.ds(width + 2, 2), rows]))
    loads.append((stiff, kext.at[pl.ds(1, width)]))
    loads.append((below.at[8], kext.at[0]))
    loads.append((above.at[8], kext.at[width + 1]))
    loads = copy_all(loads, sem)
    pad = jnp.zeros((8, 128), jnp.float32)
    for p in range(width + 4):
        for at in (0, 40):
            cext[p, pl.ds(at, 8), :] = pad
            for s in range(2):
                pres[s, p, pl.ds(at, 8), :] = pad
    for p in range(width + 2):
        for at in (0, 40):
            for s in range(2):
                mid[s, p, pl.ds(at, 8), :] = pad
    wait_all(loads)

    first = lax.axis_index("gx") * width
    background = lax.axis_index("probe") == 0
    lane = lax.broadcasted_iota(jnp.int32, (32, 128), 1)
    depth = lax.broadcasted_iota(jnp.int32, (32, 128), 0)

    def next_y(v):
        return jnp.where(lane == 127, 0.0, pltpu.roll(v, 127, 1))

    def last_y(v):
        return jnp.where(lane == 0, 0.0, pltpu.roll(v, 1, 1))

    def advance(p, src, shift, before):
        c = cext[p + shift, rows, :]
        cxp = c + cext[p + shift + 1, rows, :]
        cxm = c + cext[p + shift - 1, rows, :]
        czp = c + cext[p + shift, pl.ds(9, 32), :]
        czm = c + cext[p + shift, pl.ds(7, 32), :]
        cyp = c + next_y(c)
        cym = c + last_y(c)
        k = 0.5 * kext[p + shift - 1]
        got = []
        for s in range(2):
            v = src[s, p, rows, :]
            total = cxp * (src[s, p + 1, rows, :] - v) + cxm * (src[s, p - 1, rows, :] - v)
            total += czp * (src[s, p, pl.ds(9, 32), :] - v) + czm * (src[s, p, pl.ds(7, 32), :] - v)
            total += cyp * (next_y(v) - v) + cym * (last_y(v) - v)
            got.append(2.0 * v - before(s) + k * total)
        return got

    def inject(dst_of, planes, offset, step):
        for s in range(2):
            x = sx[s] - first + offset

            @pl.when(background & (x >= 0) & (x < planes))
            def _():
                hit = (lane == sy[s]) & (depth == sz[s])
                view = dst_of(s, x)
                view[...] = view[...] + jnp.where(hit, wavelet[s, step], 0.0)

    def step_one(p, carry):
        got = advance(p + 1, pres, 0, lambda s: prev[s, p])
        for s in range(2):
            mid[s, p, rows, :] = got[s]
        return carry

    lax.fori_loop(0, width + 2, step_one, 0)
    inject(lambda s, x: mid.at[s, x, rows], width + 2, 1, 0)
    outs = []
    for s in range(2):
        outs.append(pltpu.make_async_copy(mid.at[s, pl.ds(1, width), rows], out.at[s, 0], sem_out.at[s]))
        outs[-1].start()

    def step_two(p, carry):
        got = advance(p + 1, mid, 1, lambda s: pres[s, p + 2, rows, :])
        for s in range(2):
            o2[s, p] = got[s]
        return carry

    lax.fori_loop(0, width, step_two, 0)
    inject(lambda s, x: o2.at[s, x], width, 0, 1)
    for s in range(2):
        outs.append(pltpu.make_async_copy(o2.at[s], out.at[s, 1], sem_out.at[2 + s]))
        outs[-1].start()
    wait_all(outs)


def born_kernel(
    width, extent, xb, zb, yb, sx, sz, sy, wavelet, own, left, right, stiff, buoy, below, above, pstiff, pbuoy, fields,
    out, pieces, cext, kext, ps, pb, placed, planes, sem, sem_planes
):
    del fields
    row = lax.axis_index("probe")
    g = jnp.maximum(row - 1, 0)
    first = lax.axis_index("gx") * width
    x0 = xb[g] * EDGE - 2 - first
    rows = pl.ds(8, 32)

    @pl.when((row > 0) & (x0 < width) & (x0 + SPAN > 0))
    def _():
        loads = [(own, pieces.at[1]), (left, pieces.at[0]), (right, pieces.at[2])]
        loads.append((pstiff.at[g], ps))
        loads.append((pbuoy.at[g], pb))
        loads.append((buoy, cext.at[pl.ds(2, width), rows]))
        loads.append((below.at[pl.ds(6, 2)], cext.at[pl.ds(0, 2), rows]))
        loads.append((above.at[pl.ds(6, 2)], cext.at[pl.ds(width + 2, 2), rows]))
        loads.append((stiff, kext.at[pl.ds(2, width), rows]))
        loads.append((below.at[8], kext.at[1, rows]))
        loads.append((above.at[8], kext.at[width + 2, rows]))
        loads = copy_all(loads, sem)

        def each_plane(act):
            for i in range(SPAN):

                @pl.when((x0 + i >= 0) & (x0 + i < width))
                def _():
                    act(i)

        def fetch(i):
            return pltpu.make_async_copy(out.at[:, :, x0 + i], planes.at[i, :, :, rows], sem_planes.at[i])

        def store(i):
            return pltpu.make_async_copy(planes.at[i, :, :, rows], out.at[:, :, x0 + i], sem_planes.at[i])

        each_plane(lambda i: fetch(i).start())

        z0 = zb[g] * EDGE - 2
        y0 = yb[g] * EDGE - 2
        lane = lax.broadcasted_iota(jnp.int32, (16, 128), 1)
        depth = lax.broadcasted_iota(jnp.int32, (16, 128), 0)
        here = (lane < SPAN) & (depth < SPAN)
        here &= (lane + y0 >= 0) & (lane + y0 < 128) & (depth + z0 >= 0) & (depth + z0 < 32)
        placed[...] = jnp.zeros(placed.shape, jnp.float32)
        wait_all(loads)
        for n, values in enumerate((ps, pb)):
            placed[n, pl.ds(2, EDGE), pl.ds(2, EDGE), pl.ds(0, EDGE)] = values[...]

        def inside(i):
            x = first + x0 + i
            return (x >= 0) & (x < extent)

        def coefficient(ref, low, high):
            got = []
            for i in range(SPAN):
                at = x0 + i + 2
                ok = here & (at >= low) & (at < high)
                values = ref[jnp.clip(at, 0, width + 3), pl.ds(z0 + 8, 16), :]
                got.append(jnp.where(ok, pltpu.roll(values, wrapped(-y0), 1), 0.0))
            return jnp.stack(got)

        c = coefficient(cext, 0, width + 4)
        k = coefficient(kext, 1, width + 3)
        sb = pltpu.roll(placed[0], 2, 2)
        bb = pltpu.roll(placed[1], 2, 2)

        def piece(s, t):
            got = []
            for i in range(SPAN):
                if (s, t, i) not in STRIPS:
                    got.append(jnp.zeros((16, 128), jnp.float32))
                    continue
                n = STRIPS.index((s, t, i))
                k, q = divmod(n, PER_ROW)
                at = jnp.where(x0 + i < 0, 0, jnp.where(x0 + i < width, 1, 2))
                values = pieces[at, pl.ds(k * SPAN, 16), :]
                if q:
                    values = pltpu.roll(values, 128 - SPAN * q, 1)
                got.append(jnp.where(here & inside(i), values, 0.0))
            return jnp.stack(got)

        def up(v, axis):
            return pltpu.roll(v, v.shape[axis] - 1, axis)

        def faces(coef):
            return 0.5 * (coef[1:] + coef[:-1]), 0.5 * (coef + up(coef, 1)), 0.5 * (coef + up(coef, 2))

        def op(v, coef):
            cx, cz, cy = coef
            fx = cx * (v[1:] - v[:-1])
            fz = cz * (up(v, 1) - v)
            fy = cy * (up(v, 2) - v)
            zero = jnp.zeros((1, 16, 128), jnp.float32)
            total = jnp.concatenate([fx, zero], 0) - jnp.concatenate([zero, fx], 0)
            total += fz - pltpu.roll(fz, 1, 1)
            total += fy - pltpu.roll(fy, 1, 2)
            return total

        of_c = faces(c)
        of_b = faces(bb)
        gains = []
        for s in range(2):
            now = piece(s, 1)
            laplace = op(now, of_c)
            forcing = sb * laplace + k * op(now, of_b)
            hit = here & (lane + y0 == sy[s]) & (depth + z0 == sz[s])
            source = []
            for i in range(SPAN):
                on = hit & (first + x0 + i == sx[s])
                source.append(jnp.where(on, wavelet[s, 0], 0.0))
            later = 2.0 * now - piece(s, 0) + k * laplace + jnp.stack(source)
            second = sb * op(later, of_c) + k * op(later, of_b)
            gains.append((forcing, 2.0 * forcing + k * op(forcing, of_c) + second))
        each_plane(lambda i: fetch(i).wait())
        for s in range(2):
            for t in range(2):
                moved = pltpu.roll(gains[s][t], wrapped(y0), 2)
                for i in range(SPAN):
                    view = planes.at[i, s, t, pl.ds(z0 + 8, 16)]
                    view[...] = view[...] + moved[i]
        each_plane(lambda i: store(i).start())
        each_plane(lambda i: store(i).wait())


def on_device(
    wavefields, stiffness, buoyancy, pert_stiffness, pert_buoyancy, xblock_index, zblock_index, yblock_index,
    source_xcell, source_zcell, source_ycell, wavelet
):
    wave = wavefields[0]
    width = wave.shape[2]
    slabs = lax.axis_size("gx")
    blocks = (xblock_index, zblock_index, yblock_index)
    sources = (source_xcell, source_zcell, source_ycell, wavelet)
    f32 = functools.partial(jax.ShapeDtypeStruct, dtype=jnp.float32)
    vmem = lambda *shape: pltpu.VMEM(shape, jnp.float32)
    dma = lambda *shape: pltpu.SemaphoreType.DMA(shape)

    counts = [1 + len(rest) for rest in NEXT]
    edge = f32((9, 32, 128))
    low, high, p0, p1, p2, d0, d1, d2 = pl.pallas_call(
        functools.partial(split_kernel, width),
        out_shape=[edge, edge] + [f32((n, *PIECE)) for n in counts] + [f32(PIECE)] * 3,
        in_specs=[SMEM] * 3 + [ANY] * 3,
        out_specs=[ANY] * 8,
        scratch_shapes=[vmem(2, 2, width, 48, 128), vmem(15, *PIECE), dma(12), dma(), dma(6)],
        compiler_params=PARAMS,
        name="split",
    )(*blocks, wave, stiffness, buoyancy)

    def place(row, slab):
        return row * slabs + slab

    def along_rows(value, pairs):
        every = [(place(a, s), place(b, s)) for a, b in pairs for s in range(slabs)]
        return lax.ppermute(value, ("probe", "gx"), every)

    def along_x(value, step):
        pairs = [(s, s + step) for s in range(slabs) if 0 <= s + step < slabs]
        return lax.ppermute(value, "gx", pairs)

    firsts = [along_rows(p, [(0, row)]) for p, row in zip((p0, p1, p2), FIRST)]
    directs = [along_rows(d, [(0, row)]) for d, row in zip((d0, d1, d2), DIRECT)]
    below, above = along_x(high, 1), along_x(low, -1)
    passed = pl.pallas_call(
        pass_kernel,
        out_shape=[f32(PIECE)] * 4,
        in_specs=[ANY] * 3,
        out_specs=[ANY] * 4,
        scratch_shapes=[dma(4)],
        compiler_params=PARAMS,
        name="pass_on",
    )(*firsts)
    nexts = [
        along_rows(value, [(head, rest[n]) for head, rest in zip(FIRST, NEXT) if n < len(rest)])
        for n, value in enumerate(passed)
    ]
    advanced = pl.pallas_call(
        functools.partial(march_kernel, width),
        out_shape=f32(wave.shape),
        in_specs=[SMEM] * 4 + [ANY] * 5,
        out_specs=ANY,
        scratch_shapes=[
            vmem(2, width + 4, 48, 128),
            vmem(2, width + 2, 32, 128),
            vmem(width + 4, 48, 128),
            vmem(width + 2, 32, 128),
            vmem(2, width + 2, 48, 128),
            vmem(8, 128),
            vmem(2, width, 32, 128),
            dma(18),
            dma(4),
        ],
        compiler_params=PARAMS,
        name="march",
    )(*sources, wave, stiffness, buoyancy, below, above)
    own = pl.pallas_call(
        pick_kernel,
        out_shape=f32(PIECE),
        in_specs=[ANY] * 10,
        out_specs=ANY,
        scratch_shapes=[dma()],
        compiler_params=PARAMS,
        name="pick",
    )(*firsts, *directs, *nexts)
    left, right = along_x(own, 1), along_x(own, -1)
    result = pl.pallas_call(
        functools.partial(born_kernel, width, width * slabs),
        out_shape=f32(wave.shape),
        in_specs=[SMEM] * 7 + [ANY] * 10,
        out_specs=ANY,
        input_output_aliases={16: 0},
        scratch_shapes=[
            vmem(3, *PIECE),
            vmem(width + 4, 48, 128),
            vmem(width + 4, 48, 128),
            vmem(EDGE, EDGE, EDGE),
            vmem(EDGE, EDGE, EDGE),
            vmem(2, SPAN, 16, 128),
            vmem(SPAN, 2, 2, 48, 128),
            dma(11),
            dma(SPAN),
        ],
        compiler_params=PARAMS,
        name="born",
    )(*blocks, *sources, own, left, right, stiffness, buoyancy, below, above, pert_stiffness, pert_buoyancy, advanced)
    return result[None]


def solution(mesh):
    field = P("probe", None, None, "gx", None, None)
    return jax.shard_map(
        on_device,
        mesh=mesh,
        in_specs=(field, P("gx", None, None), P("gx", None, None)) + (P(),) * 9,
        out_specs=field,
        check_vma=False,
    )
```

```python
import functools

import jax
import jax.numpy as jnp
from jax import lax
from jax.experimental import pallas as pl
from jax.experimental.pallas import tpu as pltpu
from jax.sharding import PartitionSpec as P

EDGE = 8
SPAN = EDGE + 4
PER_ROW = 10
STRIPS = [(s, 1, i) for s in range(2) for i in range(SPAN)] + [
    (s, 0, i) for s in range(2) for i in range(1, SPAN - 1)
]
PIECE = (64, 128)

FIRST = (1, 2, 6)
NEXT = ((9, 3, 7, 5), (10, 4, 12), (14, 15))
DIRECT = (8, 11, 13)

ANY = pl.BlockSpec(memory_space=pl.ANY)
HBM = pl.BlockSpec(memory_space=pltpu.HBM)
PARAMS = pltpu.CompilerParams(vmem_limit_bytes=32 * 1024 * 1024)


def copy_all(pairs, sems, start=0):
    copies = [pltpu.make_async_copy(a, b, sems.at[start + n]) for n, (a, b) in enumerate(pairs)]
    for copy in copies:
        copy.start()
    return copies


def wait_all(copies):
    for copy in copies:
        copy.wait()


def wrapped(shift):
    return jnp.bitwise_and(shift + 128, 127)


def window(xb, zb, yb, g, first):
    return xb[g] * EDGE - 2 - first, jnp.clip(zb[g] * EDGE - 2, 0, 32 - SPAN), yb[g] * EDGE - 2


def met(x0, width):
    return (x0 < width) & (x0 + SPAN > 0)


def from_sides(swap_a, swap_b, act):
    even = lax.rem(lax.axis_index("gx"), 2) == 0

    @pl.when(even)
    def _():
        act(swap_b, swap_a)

    @pl.when(jnp.logical_not(even))
    def _():
        act(swap_a, swap_b)


def edge_kernel(width, wave, stiff, buoy, swap_a, swap_b, sem):
    def pack(low, high):
        pairs = []
        for out, outer, inner in ((low, 0, 0), (high, width - 1, width - 2)):
            for s in range(2):
                pairs.append((wave.at[s, 1, pl.ds(inner, 2)], out.at[pl.ds(2 * s, 2)]))
                pairs.append((wave.at[s, 0, outer], out.at[4 + s]))
            pairs.append((buoy.at[pl.ds(inner, 2)], out.at[pl.ds(6, 2)]))
            pairs.append((stiff.at[outer], out.at[8]))
        wait_all(copy_all(pairs, sem))

    from_sides(swap_a, swap_b, pack)


def split_kernel(
    width, xb, zb, yb, wave, swap_a, swap_b, p0, p1, p2, d0, d1, d2, sxb, szb, syb, slab, packed, sem, sem_out
):
    @pl.when(lax.axis_index("probe") == 0)
    def _():
        first = lax.axis_index("gx") * width
        index = copy_all([(xb, sxb), (zb, szb), (yb, syb)], sem)
        rows = pl.ds(0, 32)
        load = copy_all([(wave, slab.at[:, :, pl.ds(2, width), rows])], sem, 3)

        def fill(below, above):
            pairs = []
            for s in range(2):
                pairs.append((below.at[pl.ds(2 * s, 2)], slab.at[s, 1, pl.ds(0, 2), rows]))
                pairs.append((above.at[pl.ds(2 * s, 2)], slab.at[s, 1, pl.ds(width + 2, 2), rows]))
                pairs.append((below.at[4 + s], slab.at[s, 0, 1, rows]))
                pairs.append((above.at[4 + s], slab.at[s, 0, width + 2, rows]))
            wait_all(copy_all(pairs, sem, 4))

        from_sides(swap_a, swap_b, fill)
        wait_all(index)
        wait_all(load)
        lane = lax.broadcasted_iota(jnp.int32, (16, 128), 1)

        def one(g, at):
            x0, z0, y0 = window(sxb, szb, syb, g, first)

            @pl.when(met(x0, width))
            def _():
                for k in range(0, len(STRIPS), PER_ROW):
                    row = jnp.zeros((16, 128), jnp.float32)
                    for q, (s, t, i) in enumerate(STRIPS[k : k + PER_ROW]):
                        plane = jnp.clip(x0 + i + 2, 0, width + 3)
                        values = pltpu.roll(slab[s, t, plane, pl.ds(z0, 16), :], wrapped(SPAN * q - y0), 1)
                        row = jnp.where((lane >= SPAN * q) & (lane < SPAN * (q + 1)), values, row)
                    packed[at, pl.ds(k // PER_ROW * SPAN, 16), :] = row

        spots = []
        for head, rest in zip(FIRST, NEXT):
            spots += [head, *rest]
        spots += DIRECT
        for at, row in enumerate(spots):
            one(row - 1, at)

        outs, at = [], 0
        for out, rest in zip((p0, p1, p2), NEXT):
            outs.append((packed.at[pl.ds(at, 1 + len(rest))], out))
            at += 1 + len(rest)
        for out in (d0, d1, d2):
            outs.append((packed.at[at], out))
            at += 1
        wait_all(copy_all(outs, sem_out))


def pass_kernel(r0, r1, r2, after, q0, q1, q2, q3, sem):
    del after
    row = lax.axis_index("probe")
    for head, rest, got in zip(FIRST, NEXT, (r0, r1, r2)):

        @pl.when(row == head)
        def _():
            pairs = [(got.at[1 + n], out) for n, out in zip(range(len(rest)), (q0, q1, q2, q3))]
            wait_all(copy_all(pairs, sem))


def march_kernel(
    width, xb, zb, yb, sx, sz, sy, wavelet, wave, stiff, buoy, swap_a, swap_b, pstiff, pbuoy, out, prep,
    sxb, szb, syb, ssx, ssz, ssy, swavelet, pres, prev, cext, kext, mid, later, perts, placed, sem, sem_side, sem_out,
):
    rows = pl.ds(8, 32)
    scalars = [(xb, sxb), (zb, szb), (yb, syb), (sx, ssx), (sz, ssz), (sy, ssy), (wavelet, swavelet)]
    loads = copy_all(scalars, sem)
    bulk = [(buoy, cext.at[pl.ds(2, width), rows]), (stiff, kext.at[pl.ds(2, width), pl.ds(0, 32)])]
    for s in range(2):
        bulk.append((wave.at[s, 1], pres.at[s, pl.ds(2, width), rows]))
        bulk.append((wave.at[s, 0], prev.at[s, pl.ds(1, width)]))
    bulk += [(pstiff, perts.at[0]), (pbuoy, perts.at[1])]
    loads += copy_all(bulk, sem, len(scalars))
    pad = jnp.zeros((8, 128), jnp.float32)
    for p in range(width + 4):
        for at in (0, 40):
            cext[p, pl.ds(at, 8), :] = pad
            for s in range(2):
                pres[s, p, pl.ds(at, 8), :] = pad
    for p in range(width + 2):
        for at in (0, 40):
            for s in range(2):
                mid[s, p, pl.ds(at, 8), :] = pad

    def fill(below, above):
        pairs = []
        for s in range(2):
            pairs.append((below.at[pl.ds(2 * s, 2)], pres.at[s, pl.ds(0, 2), rows]))
            pairs.append((above.at[pl.ds(2 * s, 2)], pres.at[s, pl.ds(width + 2, 2), rows]))
            pairs.append((below.at[4 + s], prev.at[s, 0]))
            pairs.append((above.at[4 + s], prev.at[s, width + 1]))
        pairs.append((below.at[pl.ds(6, 2)], cext.at[pl.ds(0, 2), rows]))
        pairs.append((above.at[pl.ds(6, 2)], cext.at[pl.ds(width + 2, 2), rows]))
        pairs.append((below.at[8], kext.at[1, pl.ds(0, 32)]))
        pairs.append((above.at[8], kext.at[width + 2, pl.ds(0, 32)]))
        wait_all(copy_all(pairs, sem_side))

    from_sides(swap_a, swap_b, fill)
    wait_all(loads)

    first = lax.axis_index("gx") * width
    row = lax.axis_index("probe")
    lane = lax.broadcasted_iota(jnp.int32, (32, 128), 1)
    depth = lax.broadcasted_iota(jnp.int32, (32, 128), 0)

    def next_y(v):
        return jnp.where(lane == 127, 0.0, pltpu.roll(v, 127, 1))

    def last_y(v):
        return jnp.where(lane == 0, 0.0, pltpu.roll(v, 1, 1))

    def advance(p, src, shift, before):
        c = cext[p + shift, rows, :]
        cxp = c + cext[p + shift + 1, rows, :]
        cxm = c + cext[p + shift - 1, rows, :]
        czp = c + cext[p + shift, pl.ds(9, 32), :]
        czm = c + cext[p + shift, pl.ds(7, 32), :]
        cyp = c + next_y(c)
        cym = c + last_y(c)
        k = 0.5 * kext[p + shift, pl.ds(0, 32), :]
        got = []
        for s in range(2):
            v = src[s, p, rows, :]
            total = cxp * (src[s, p + 1, rows, :] - v) + cxm * (src[s, p - 1, rows, :] - v)
            total += czp * (src[s, p, pl.ds(9, 32), :] - v) + czm * (src[s, p, pl.ds(7, 32), :] - v)
            total += cyp * (next_y(v) - v) + cym * (last_y(v) - v)
            got.append(2.0 * v - before(s) + k * total)
        return got

    def inject(view_of, planes, offset, step):
        for s in range(2):
            x = ssx[s] - first + offset

            @pl.when((row == 0) & (x >= 0) & (x < planes))
            def _():
                hit = (lane == ssy[s]) & (depth == ssz[s])
                view = view_of(s, x)
                view[...] = view[...] + jnp.where(hit, swavelet[s, step], 0.0)

    def step_one(p, carry):
        got = advance(p + 1, pres, 0, lambda s: prev[s, p])
        for s in range(2):
            mid[s, p, rows, :] = got[s]
        return carry

    lax.fori_loop(0, width + 2, step_one, 0)
    inject(lambda s, x: mid.at[s, x, rows], width + 2, 1, 0)
    outs = copy_all([(mid.at[s, pl.ds(1, width), rows], out.at[s, 0]) for s in range(2)], sem_out)

    def step_two(p, carry):
        got = advance(p + 1, mid, 1, lambda s: pres[s, p + 2, rows, :])
        for s in range(2):
            later[s, p] = got[s]
        return carry

    lax.fori_loop(0, width, step_two, 0)
    inject(lambda s, x: later.at[s, x], width, 0, 1)
    outs += copy_all([(later.at[s], out.at[s, 1]) for s in range(2)], sem_out, 2)

    g = jnp.maximum(row - 1, 0)
    x0, z0, y0 = window(sxb, szb, syb, g, first)

    @pl.when((row > 0) & met(x0, width))
    def _():
        strip = lax.broadcasted_iota(jnp.int32, (16, 128), 1)
        here = (strip < SPAN) & (lax.broadcasted_iota(jnp.int32, (16, 128), 0) < SPAN)
        here &= (strip + y0 >= 0) & (strip + y0 < 128)
        placed[...] = jnp.zeros(placed.shape, jnp.float32)
        for n, (ref, top, low) in enumerate(((cext, 8, 0), (kext, 0, 1))):
            for i in range(SPAN):
                at = x0 + i + 2
                ok = here & (at >= low) & (at < width + 4 - low)
                values = ref[jnp.clip(at, 0, width + 3), pl.ds(z0 + top, 16), :]
                placed[n, i] = jnp.where(ok, pltpu.roll(values, wrapped(-y0), 1), 0.0)
        wide = lax.broadcasted_iota(jnp.int32, (EDGE, EDGE, perts.shape[-1]), 2)
        diagonal = lax.broadcasted_iota(jnp.int32, (EDGE, EDGE, 128), 2)
        diagonal = diagonal == lax.broadcasted_iota(jnp.int32, (EDGE, EDGE, 128), 1) + 2
        dz = szb[g] * EDGE - z0
        for n in range(2):
            for i in range(EDGE):
                column = jnp.sum(jnp.where(wide == g, perts[n, i], 0.0), axis=2, keepdims=True)
                block = jnp.sum(jnp.where(diagonal, column, 0.0), axis=1)
                placed[2 + n, 2 + i, pl.ds(dz, EDGE), :] = block
        wait_all(copy_all([(placed, prep)], sem_out, 4))

    wait_all(outs)


def born_kernel(
    width, extent, xb, zb, yb, sx, sz, sy, wavelet, r0, r1, r2, d0, d1, d2, q0, q1, q2, q3, prep, fields, out,
    sxb, szb, syb, ssx, ssz, ssy, swavelet, piece, placed, planes, sem, sem_planes,
):
    del fields
    row = lax.axis_index("probe")

    @pl.when(row > 0)
    def _():
        scalars = [(xb, sxb), (zb, szb), (yb, syb), (sx, ssx), (sz, ssz), (sy, ssy), (wavelet, swavelet)]
        wait_all(copy_all(scalars, sem))
        g = row - 1
        first = lax.axis_index("gx") * width
        x0, z0, y0 = window(sxb, szb, syb, g, first)

        @pl.when(met(x0, width))
        def _():
            load = copy_all([(prep, placed)], sem)

            def each_plane(act):
                for i in range(SPAN):

                    @pl.when((x0 + i >= 0) & (x0 + i < width))
                    def _():
                        act(i)

            def plane(i):
                return out.at[:, :, x0 + i], planes.at[i, :, :, pl.ds(0, 32)]

            def fetch(i):
                source, target = plane(i)
                return pltpu.make_async_copy(source, target, sem_planes.at[i])

            def store(i):
                target, source = plane(i)
                return pltpu.make_async_copy(source, target, sem_planes.at[i])

            each_plane(lambda i: fetch(i).start())

            def bring(where, source):
                @pl.when(where)
                def _():
                    wait_all(copy_all([(source, piece)], sem, 1))

            for head, got in zip(FIRST, (r0, r1, r2)):
                bring(row == head, got.at[0])
            for target, got in zip(DIRECT, (d0, d1, d2)):
                bring(row == target, got)
            for n, got in enumerate((q0, q1, q2, q3)):
                where = row < 0
                for rest in NEXT:
                    if n < len(rest):
                        where = where | (row == rest[n])
                bring(where, got)
            wait_all(load)

            lane = lax.broadcasted_iota(jnp.int32, (16, 128), 1)
            depth = lax.broadcasted_iota(jnp.int32, (16, 128), 0)
            here = (lane < SPAN) & (depth < SPAN) & (lane + y0 >= 0) & (lane + y0 < 128)
            c, k, sb, bb = (placed[n] for n in range(4))

            def field(s, t):
                got = []
                for i in range(SPAN):
                    if (s, t, i) not in STRIPS:
                        got.append(jnp.zeros((16, 128), jnp.float32))
                        continue
                    at, q = divmod(STRIPS.index((s, t, i)), PER_ROW)
                    values = piece[pl.ds(at * SPAN, 16), :]
                    if q:
                        values = pltpu.roll(values, 128 - SPAN * q, 1)
                    x = x0 + i
                    ok = here & (first + x >= 0) & (first + x < extent)
                    ok &= (x >= -1 - t) & (x < width + 1 + t)
                    got.append(jnp.where(ok, values, 0.0))
                return jnp.stack(got)

            def up(v, axis):
                return pltpu.roll(v, v.shape[axis] - 1, axis)

            def faces(coef):
                return 0.5 * (coef[1:] + coef[:-1]), 0.5 * (coef + up(coef, 1)), 0.5 * (coef + up(coef, 2))

            def op(v, coef):
                cx, cz, cy = coef
                fx = cx * (v[1:] - v[:-1])
                fz = cz * (up(v, 1) - v)
                fy = cy * (up(v, 2) - v)
                zero = jnp.zeros((1, 16, 128), jnp.float32)
                total = jnp.concatenate([fx, zero], 0) - jnp.concatenate([zero, fx], 0)
                total += fz - pltpu.roll(fz, 1, 1)
                total += fy - pltpu.roll(fy, 1, 2)
                return total

            of_c = faces(c)
            of_b = faces(bb)
            gains = []
            for s in range(2):
                now = field(s, 1)
                laplace = op(now, of_c)
                forcing = sb * laplace + k * op(now, of_b)
                hit = here & (lane + y0 == ssy[s]) & (depth + z0 == ssz[s])
                source = []
                for i in range(SPAN):
                    on = hit & (first + x0 + i == ssx[s])
                    source.append(jnp.where(on, swavelet[s, 0], 0.0))
                later = 2.0 * now - field(s, 0) + k * laplace + jnp.stack(source)
                second = sb * op(later, of_c) + k * op(later, of_b)
                gains.append((forcing, 2.0 * forcing + k * op(forcing, of_c) + second))
            each_plane(lambda i: fetch(i).wait())
            for s in range(2):
                for t in range(2):
                    moved = pltpu.roll(gains[s][t], wrapped(y0), 2)
                    for i in range(SPAN):
                        view = planes.at[i, s, t, pl.ds(z0, 16)]
                        view[...] = view[...] + moved[i]
            each_plane(lambda i: store(i).start())
            each_plane(lambda i: store(i).wait())


def on_device(
    wavefields, stiffness, buoyancy, pert_stiffness, pert_buoyancy, xblock_index, zblock_index, yblock_index,
    source_xcell, source_zcell, source_ycell, wavelet
):
    wave = wavefields[0]
    width = wave.shape[2]
    slabs = lax.axis_size("gx")
    blocks = (xblock_index, zblock_index, yblock_index)
    sources = (source_xcell, source_zcell, source_ycell, wavelet)
    perts = [jnp.transpose(p, (1, 2, 3, 0)) for p in (pert_stiffness, pert_buoyancy)]
    f32 = functools.partial(jax.ShapeDtypeStruct, dtype=jnp.float32)
    vmem = lambda *shape: pltpu.VMEM(shape, jnp.float32)
    dma = lambda *shape: pltpu.SemaphoreType.DMA(shape)
    in_smem = lambda arrays: [pltpu.SMEM(a.shape, a.dtype) for a in arrays]

    def call(kernel, name, out_shape, in_specs, scratch, **more):
        made = pl.pallas_call(
            kernel,
            out_shape=out_shape,
            in_specs=in_specs,
            out_specs=jax.tree.map(lambda _: ANY, out_shape),
            scratch_shapes=scratch,
            compiler_params=PARAMS,
            name=name,
            **more,
        )

        def run(*args):
            keep = lambda x: pltpu.with_memory_space_constraint(x, pltpu.HBM)
            return made(*(keep(x) if spec is HBM else x for x, spec in zip(args, in_specs)))

        return run

    def along_rows(value, pairs):
        every = [(a * slabs + s, b * slabs + s) for a, b in pairs for s in range(slabs)]
        return lax.ppermute(value, ("probe", "gx"), every)

    def swap(value, start):
        pairs = [(s, s + 1) for s in range(start, slabs - 1, 2)]
        return lax.ppermute(value, "gx", pairs + [(b, a) for a, b in pairs])

    edge = f32((9, 32, 128))
    edge_a, edge_b = call(
        functools.partial(edge_kernel, width), "edges", [edge, edge], [HBM] * 3, [dma(12)]
    )(wave, stiffness, buoyancy)
    swap_b, swap_a = swap(edge_b, 1), swap(edge_a, 0)

    counts = [1 + len(rest) for rest in NEXT]
    p0, p1, p2, d0, d1, d2 = call(
        functools.partial(split_kernel, width),
        "split",
        [f32((n, *PIECE)) for n in counts] + [f32(PIECE)] * 3,
        [HBM] * 4 + [ANY] * 2,
        [*in_smem(blocks), vmem(2, 2, width + 4, 40, 128), vmem(15, *PIECE), dma(12), dma(6)],
    )(*blocks, wave, swap_a, swap_b)
    firsts = [along_rows(p, [(0, row)]) for p, row in zip((p0, p1, p2), FIRST)]
    directs = [along_rows(d, [(0, row)]) for d, row in zip((d0, d1, d2), DIRECT)]

    advanced, prep = call(
        functools.partial(march_kernel, width),
        "march",
        [f32(wave.shape), f32((4, SPAN, 16, 128))],
        [HBM] * 10 + [ANY] * 2 + [HBM] * 2,
        [
            *in_smem(blocks + sources),
            vmem(2, width + 4, 48, 128),
            vmem(2, width + 2, 32, 128),
            vmem(width + 4, 48, 128),
            vmem(width + 4, 40, 128),
            vmem(2, width + 2, 48, 128),
            vmem(2, width, 32, 128),
            vmem(2, *perts[0].shape),
            vmem(4, SPAN, 16, 128),
            dma(15),
            dma(12),
            dma(5),
        ],
    )(*blocks, *sources, wave, stiffness, buoyancy, swap_a, swap_b, *perts)

    passed = call(pass_kernel, "pass_on", [f32(PIECE)] * 4, [ANY] * 4, [dma(4)])(*firsts, prep)
    nexts = [
        along_rows(value, [(head, rest[n]) for head, rest in zip(FIRST, NEXT) if n < len(rest)])
        for n, value in enumerate(passed)
    ]
    result = call(
        functools.partial(born_kernel, width, width * slabs),
        "born",
        f32(wave.shape),
        [HBM] * 7 + [ANY] * 12,
        [
            *in_smem(blocks + sources),
            vmem(*PIECE),
            vmem(4, SPAN, 16, 128),
            vmem(SPAN, 2, 2, 40, 128),
            dma(7),
            dma(SPAN),
        ],
        input_output_aliases={18: 0},
    )(*blocks, *sources, *firsts, *directs, *nexts, prep, advanced)
    return result[None]


def solution(mesh):
    field = P("probe", None, None, "gx", None, None)
    return jax.shard_map(
        on_device,
        mesh=mesh,
        in_specs=(field, P("gx", None, None), P("gx", None, None)) + (P(),) * 9,
        out_specs=field,
        check_vma=False,
    )
```

```python
import functools

import jax
import jax.numpy as jnp
from jax import lax
from jax.experimental import pallas as pl
from jax.experimental.pallas import tpu as pltpu
from jax.sharding import PartitionSpec as P

EDGE = 8
SPAN = EDGE + 4
DEPTH = 32
PER_ROW = 10
STRIPS = [(s, 1, i) for s in range(2) for i in range(SPAN)] + [
    (s, 0, i) for s in range(2) for i in range(1, SPAN - 1)
]
ROWS = 64

FIRST = (1, 2, 6, 8)
NEXT = ((9, 3, 7, 5), (10, 4, 12), (14, 15), (11,))
DIRECT = (13,)

PARAMS = pltpu.CompilerParams(vmem_limit_bytes=32 * 1024 * 1024)


def copy_all(pairs, sems, start=0):
    copies = [pltpu.make_async_copy(a, b, sems.at[start + n]) for n, (a, b) in enumerate(pairs)]
    for copy in copies:
        copy.start()
    return copies


def wait_all(copies):
    for copy in copies:
        copy.wait()


def wrapped(shift):
    return jnp.bitwise_and(shift + 128, 127)


def plane_rows(p, count=1):
    start = p * DEPTH
    return pl.ds(start if isinstance(p, int) else pl.multiple_of(start, DEPTH), count * DEPTH)


def window(blocks, g, first):
    xb, zb, yb = blocks
    return xb[g] * EDGE - 2 - first, jnp.clip(zb[g] * EDGE - 2, 0, DEPTH - SPAN), yb[g] * EDGE - 2


def met(x0, width):
    return (x0 < width) & (x0 + SPAN > 0)


def from_sides(swap_a, swap_b, act):
    even = lax.rem(lax.axis_index("gx"), 2) == 0

    @pl.when(even)
    def _():
        act(swap_b, swap_a)

    @pl.when(jnp.logical_not(even))
    def _():
        act(swap_a, swap_b)


def edge_kernel(width, wave, stiff, buoy, swap_a, swap_b, sem):
    def pack(low, high):
        pairs = []
        for out, outer, inner in ((low, 0, 0), (high, width - 1, width - 2)):
            for s in range(2):
                pairs.append((wave.at[s, 1, plane_rows(inner, 2)], out.at[plane_rows(2 * s, 2)]))
                pairs.append((wave.at[s, 0, plane_rows(outer)], out.at[plane_rows(4 + s)]))
            pairs.append((buoy.at[plane_rows(inner, 2)], out.at[plane_rows(6, 2)]))
            pairs.append((stiff.at[plane_rows(outer)], out.at[plane_rows(8)]))
        wait_all(copy_all(pairs, sem))

    from_sides(swap_a, swap_b, pack)


def keep_sides(swap_a, swap_b, sides):
    def act(below, above):
        sides[0] = below[...]
        sides[1] = above[...]

    from_sides(swap_a, swap_b, act)


def split_kernel(width, xb, zb, yb, wave, swap_a, swap_b, *refs):
    outs, sides = refs[:-1], refs[-1]
    packs = [(head, *rest) for head, rest in zip(FIRST, NEXT)] + [(row,) for row in DIRECT]

    @pl.when(lax.axis_index("probe") == 0)
    def _():
        first = lax.axis_index("gx") * width
        keep_sides(swap_a, swap_b, sides)
        lane = lax.broadcasted_iota(jnp.int32, (8, 128), 1)

        def cut(g, out, at):
            x0, z0, y0 = window((xb, zb, yb), g, first)

            def place(n, load):
                k, q = divmod(n, PER_ROW)
                for half in (0, SPAN - 8):
                    spot = pl.ds(at * ROWS + k * SPAN + half, 8)
                    values = pltpu.roll(load(half), wrapped(SPAN * q - y0), 1)
                    mine = (lane >= SPAN * q) & (lane < SPAN * (q + 1))
                    out[spot, :] = jnp.where(mine, values, out[spot, :])

            @pl.when(met(x0, width))
            def _():
                for i in range(SPAN):
                    p = x0 + i
                    strips = [(n, s, t) for n, (s, t, j) in enumerate(STRIPS) if j == i]

                    @pl.when((p >= 0) & (p < width))
                    def _():
                        for n, s, t in strips:
                            place(n, lambda half: wave[s, t, pl.ds(p * DEPTH + z0 + half, 8), :])

                    @pl.when(((p >= -2) & (p < 0)) | ((p >= width) & (p < width + 2)))
                    def _():
                        side = jnp.where(p < 0, 0, 1)
                        j = jnp.where(p < 0, p + 2, p - width)
                        for n, s, t in strips:
                            top = (2 * s + j if t else 4 + s) * DEPTH + z0
                            place(n, lambda half: sides[side, pl.ds(top + half, 8), :])

        for out, members in zip(outs, packs):

            def each(at, carry):
                row = jnp.int32(members[0])
                for n, member in enumerate(members[1:], 1):
                    row = jnp.where(at == n, member, row)
                cut(row - 1, out, at)
                return carry

            lax.fori_loop(0, len(members), each, 0)


def pass_kernel(*refs):
    got, outs = refs[: len(FIRST)], refs[len(FIRST) + 1 :]
    row = lax.axis_index("probe")
    for head, rest, source in zip(FIRST, NEXT, got):

        @pl.when(row == head)
        def _():
            for n, out in zip(range(len(rest)), outs):
                out[...] = source[pl.ds((1 + n) * ROWS, ROWS), :]


def march_kernel(
    width, xb, zb, yb, sx, sz, sy, wavelet, wave, stiff, buoy, swap_a, swap_b, pstiff, pbuoy, out, prep, fields,
    sides, mid, later, weights, sem_out,
):
    first = lax.axis_index("gx") * width
    row = lax.axis_index("probe")
    keep_sides(swap_a, swap_b, sides)
    lane = lax.broadcasted_iota(jnp.int32, (DEPTH, 128), 1)
    depth = lax.broadcasted_iota(jnp.int32, (DEPTH, 128), 0)
    top, bottom = depth == 0, depth == DEPTH - 1
    left, right = lane == 0, lane == 127

    def present(s, p):
        if isinstance(p, int) and p < 0:
            return sides[0, plane_rows(2 * s + p + 2), :]
        if isinstance(p, int) and p >= width:
            return sides[1, plane_rows(2 * s + p - width), :]
        return wave[s, 1, plane_rows(p), :]

    def earlier(s, p):
        if isinstance(p, int) and (p < 0 or p >= width):
            return sides[0 if p < 0 else 1, plane_rows(4 + s), :]
        return wave[s, 0, plane_rows(p), :]

    def coefficients(p):
        if isinstance(p, int) and (p < 0 or p >= width):
            side = 0 if p < 0 else 1
            return sides[side, plane_rows(6 + (p + 2 if p < 0 else p - width)), :], sides[side, plane_rows(8), :]
        return buoy[plane_rows(p), :], stiff[plane_rows(p), :]

    def weigh(c, cxm, cxp, czm, czp, k):
        k = 0.5 * k
        edge = k * c
        wide = [k * (c + cxm), k * (c + cxp)]
        total = wide[0] + wide[1]
        for value, outside in (
            (czm, top),
            (czp, bottom),
            (pltpu.roll(c, 1, 1), left),
            (pltpu.roll(c, 127, 1), right),
        ):
            full = k * (c + value)
            total += jnp.where(outside, edge, full)
            wide.append(jnp.where(outside, 0.0, full))
        return wide + [2.0 - total]

    def weighted(w, v, vxm, vxp, vzm, vzp, before):
        near = (w[0] * vxm + w[1] * vxp) + (w[2] * vzm + w[3] * vzp)
        near += w[4] * pltpu.roll(v, 1, 1) + w[5] * pltpu.roll(v, 127, 1)
        return (w[6] * v - before) + near

    def save(w, p):
        for n in range(7):
            weights[n, plane_rows(p), :] = w[n]

    def up(v):
        return pltpu.roll(v, 1, 0)

    def down(v):
        return pltpu.roll(v, DEPTH - 1, 0)

    for p in (-1, 0, width - 1, width):
        c, k = coefficients(p)
        w = weigh(c, coefficients(p - 1)[0], coefficients(p + 1)[0], up(c), down(c), k)
        if 0 <= p < width:
            save(w, p)
        for s in range(2):
            v = present(s, p)
            mid[s, plane_rows(p + 1), :] = weighted(
                w, v, present(s, p - 1), present(s, p + 1), up(v), down(v), earlier(s, p)
            )

    def step_one(p, carry):
        above, below = pl.ds(p * DEPTH - 1, DEPTH), pl.ds(p * DEPTH + 1, DEPTH)
        c, k = coefficients(p)
        w = weigh(c, buoy[plane_rows(p - 1), :], buoy[plane_rows(p + 1), :], buoy[above, :], buoy[below, :], k)
        save(w, p)
        for s in range(2):
            mid[s, plane_rows(p + 1), :] = weighted(
                w, present(s, p), present(s, p - 1), present(s, p + 1), wave[s, 1, above, :], wave[s, 1, below, :],
                earlier(s, p),
            )
        return carry

    lax.fori_loop(1, width - 1, step_one, 0)

    def inject(ref, step, low, high, shift):
        for s in range(2):
            x = sx[s] - first

            @pl.when((row == 0) & (x >= low) & (x < high))
            def _():
                hit = (lane == sy[s]) & (depth == sz[s])
                spot = plane_rows(x + shift)
                ref[s, spot, :] = ref[s, spot, :] + jnp.where(hit, wavelet[s, step], 0.0)

    inject(mid, 0, -1, width + 1, 1)
    outs = copy_all([(mid.at[s, plane_rows(1, width)], out.at[s, 0]) for s in range(2)], sem_out)

    def step_two(p, carry):
        above, below = pl.ds((p + 1) * DEPTH - 1, DEPTH), pl.ds((p + 1) * DEPTH + 1, DEPTH)
        w = [weights[n, plane_rows(p), :] for n in range(7)]
        for s in range(2):
            later[s, plane_rows(p), :] = weighted(
                w, mid[s, plane_rows(p + 1), :], mid[s, plane_rows(p), :], mid[s, plane_rows(p + 2), :],
                mid[s, above, :], mid[s, below, :], present(s, p),
            )
        return carry

    part = width // 3
    for n in range(3):
        low, high = n * part, (n + 1) * part
        lax.fori_loop(low, high, step_two, 0)
        inject(later, 1, low, high, 0)
        pairs = [(later.at[s, plane_rows(low, part)], out.at[s, 1, plane_rows(low, part)]) for s in range(2)]
        outs += copy_all(pairs, sem_out, 2 + 2 * n)

    g = jnp.maximum(row - 1, 0)
    x0, z0, y0 = window((xb, zb, yb), g, first)

    @pl.when((row > 0) & met(x0, width))
    def _():
        strip = lax.broadcasted_iota(jnp.int32, (8, 128), 1)
        here = (strip < SPAN) & (strip + y0 >= 0) & (strip + y0 < 128)
        prep[...] = jnp.zeros(prep.shape, jnp.float32)

        def bring(n, i, load):
            for half in (0, SPAN - 8):
                prep[n, i, pl.ds(half, 8), :] = jnp.where(here, pltpu.roll(load(half), wrapped(-y0), 1), 0.0)

        for i in range(SPAN):
            p = x0 + i

            @pl.when((p >= 0) & (p < width))
            def _():
                bring(0, i, lambda half: buoy[pl.ds(p * DEPTH + z0 + half, 8), :])
                bring(1, i, lambda half: stiff[pl.ds(p * DEPTH + z0 + half, 8), :])
                for s in range(2):
                    fields[i, s, 0] = mid[s, plane_rows(p + 1), :]
                    fields[i, s, 1] = later[s, plane_rows(p), :]

            side = jnp.where(p < 0, 0, 1)
            j = jnp.where(p < 0, p + 2, p - width)

            @pl.when(((p >= -2) & (p < 0)) | ((p >= width) & (p < width + 2)))
            def _():
                bring(0, i, lambda half: sides[side, pl.ds((6 + j) * DEPTH + z0 + half, 8), :])

            @pl.when((p == -1) | (p == width))
            def _():
                bring(1, i, lambda half: sides[side, pl.ds(8 * DEPTH + z0 + half, 8), :])

        wide = lax.broadcasted_iota(jnp.int32, (EDGE, EDGE, pstiff.shape[-1]), 2)
        diagonal = lax.broadcasted_iota(jnp.int32, (EDGE, EDGE, 128), 2)
        diagonal = diagonal == lax.broadcasted_iota(jnp.int32, (EDGE, EDGE, 128), 1) + 2
        dz = zb[g] * EDGE - z0
        for n, ref in ((2, pstiff), (3, pbuoy)):
            for i in range(EDGE):
                column = jnp.sum(jnp.where(wide == g, ref[i], 0.0), axis=2, keepdims=True)
                prep[n, 2 + i, pl.ds(dz, EDGE), :] = jnp.sum(jnp.where(diagonal, column, 0.0), axis=1)

    wait_all(outs)


def born_kernel(width, extent, xb, zb, yb, sx, sz, sy, wavelet, *refs):
    count = len(FIRST) + len(DIRECT)
    longest = max(len(rest) for rest in NEXT)
    firsts, directs, nexts = refs[: len(FIRST)], refs[len(FIRST) : count], refs[count : count + longest]
    prep, fields, _, out, piece, planes, sem = refs[count + longest :]
    row = lax.axis_index("probe")
    g = jnp.maximum(row - 1, 0)
    first = lax.axis_index("gx") * width
    x0, z0, y0 = window((xb, zb, yb), g, first)

    @pl.when((row > 0) & met(x0, width))
    def _():
        def bring(where, source):
            @pl.when(where)
            def _():
                piece[...] = source[pl.ds(0, ROWS), :]

        for target, source in zip(FIRST + DIRECT, (*firsts, *directs)):
            bring(row == target, source)
        for n, source in enumerate(nexts):
            where = row < 0
            for rest in NEXT:
                if n < len(rest):
                    where = where | (row == rest[n])
            bring(where, source)

        lane = lax.broadcasted_iota(jnp.int32, (16, 128), 1)
        depth = lax.broadcasted_iota(jnp.int32, (16, 128), 0)
        here = (lane < SPAN) & (depth < SPAN) & (lane + y0 >= 0) & (lane + y0 < 128)
        c, k, sb, bb = (prep[n] for n in range(4))

        def field(s, t):
            got = []
            for i in range(SPAN):
                if (s, t, i) not in STRIPS:
                    got.append(jnp.zeros((16, 128), jnp.float32))
                    continue
                at, q = divmod(STRIPS.index((s, t, i)), PER_ROW)
                values = piece[pl.ds(at * SPAN, 16), :]
                if q:
                    values = pltpu.roll(values, 128 - SPAN * q, 1)
                x = x0 + i
                ok = (first + x >= 0) & (first + x < extent) & (x >= -1 - t) & (x < width + 1 + t)
                got.append(jnp.where(here & ok, values, 0.0))
            return jnp.stack(got)

        def up(v, axis):
            return pltpu.roll(v, v.shape[axis] - 1, axis)

        def faces(coef):
            return 0.5 * (coef[1:] + coef[:-1]), 0.5 * (coef + up(coef, 1)), 0.5 * (coef + up(coef, 2))

        def steps(v):
            return v[1:] - v[:-1], up(v, 1) - v, up(v, 2) - v

        def gather(coef, step):
            fx, fz, fy = (a * b for a, b in zip(coef, step))
            zero = jnp.zeros((1, 16, 128), jnp.float32)
            total = jnp.concatenate([fx, zero], 0) - jnp.concatenate([zero, fx], 0)
            total += fz - pltpu.roll(fz, 1, 1)
            total += fy - pltpu.roll(fy, 1, 2)
            return total

        of_c = faces(c)
        of_b = faces(bb)
        for s in range(2):
            now = field(s, 1)
            step = steps(now)
            laplace = gather(of_c, step)
            forcing = sb * laplace + k * gather(of_b, step)
            hit = here & (lane + y0 == sy[s]) & (depth + z0 == sz[s])
            source = []
            for i in range(SPAN):
                on = hit & (first + x0 + i == sx[s])
                source.append(jnp.where(on, wavelet[s, 0], 0.0))
            then = steps(2.0 * now - field(s, 0) + k * laplace + jnp.stack(source))
            second = sb * gather(of_c, then) + k * gather(of_b, then)
            gains = (forcing, 2.0 * forcing + k * gather(of_c, steps(forcing)) + second)
            for t in range(2):
                moved = pltpu.roll(gains[t], wrapped(y0), 2)
                for i in range(SPAN):
                    planes[i, s, t, pl.ds(0, DEPTH), :] = fields[i, s, t]
                    spot = pl.ds(z0, 16)
                    planes[i, s, t, spot, :] = planes[i, s, t, spot, :] + moved[i]

        def each_plane(act):
            for i in range(SPAN):

                @pl.when((x0 + i >= 0) & (x0 + i < width))
                def _():
                    target = out.at[:, :, plane_rows(x0 + i)]
                    act(pltpu.make_async_copy(planes.at[i, :, :, pl.ds(0, DEPTH)], target, sem.at[i]))

        each_plane(lambda copy: copy.start())
        each_plane(lambda copy: copy.wait())


def on_device(
    wavefields, stiffness, buoyancy, pert_stiffness, pert_buoyancy, xblock_index, zblock_index, yblock_index,
    source_xcell, source_zcell, source_ycell, wavelet
):
    width = wavefields.shape[3]
    slabs = lax.axis_size("gx")
    rows = width * DEPTH
    wave = wavefields.reshape(2, 2, rows, 128)
    stiff, buoy = stiffness.reshape(rows, 128), buoyancy.reshape(rows, 128)
    blocks = (xblock_index, zblock_index, yblock_index)
    sources = (source_xcell, source_zcell, source_ycell, wavelet)
    perts = [jnp.transpose(p, (1, 2, 3, 0)) for p in (pert_stiffness, pert_buoyancy)]
    hbm = lambda *shape: pltpu.HBM(shape, jnp.float32)
    vmem = lambda *shape: pltpu.VMEM(shape, jnp.float32)
    dma = lambda *shape: pltpu.SemaphoreType.DMA(shape)

    def call(kernel, name, out_shape, spaces, scratch, **more):
        made = pl.pallas_call(
            kernel,
            out_shape=out_shape,
            in_specs=[pl.BlockSpec(memory_space=space) for space in spaces],
            out_specs=jax.tree.map(lambda s: pl.BlockSpec(memory_space=s.memory_space), out_shape),
            scratch_shapes=scratch,
            compiler_params=PARAMS,
            name=name,
            **more,
        )
        return lambda *args: made(*map(pltpu.with_memory_space_constraint, args, spaces))

    def along_rows(value, pairs):
        every = [(a * slabs + s, b * slabs + s) for a, b in pairs for s in range(slabs)]
        return lax.ppermute(value, ("probe", "gx"), every)

    def swap(value, start):
        pairs = [(s, s + 1) for s in range(start, slabs - 1, 2)]
        return lax.ppermute(value, "gx", pairs + [(b, a) for a, b in pairs])

    smem = pltpu.SMEM
    edge = vmem(9 * DEPTH, 128)
    edge_a, edge_b = call(
        functools.partial(edge_kernel, width), "edges", [edge, edge], [pltpu.HBM] * 3, [dma(12)]
    )(wave, stiff, buoy)
    swap_a, swap_b = swap(edge_a, 0), swap(edge_b, 1)

    counts = [1 + len(rest) for rest in NEXT] + [1] * len(DIRECT)
    packs = call(
        functools.partial(split_kernel, width),
        "split",
        [vmem(n * ROWS, 128) for n in counts],
        [smem] * 3 + [pltpu.VMEM] * 3,
        [vmem(2, 9 * DEPTH, 128)],
    )(*blocks, wave, swap_a, swap_b)
    got = [along_rows(p, [(0, row)]) for p, row in zip(packs, FIRST + DIRECT)]

    advanced, prep, fields = call(
        functools.partial(march_kernel, width),
        "march",
        [hbm(2, 2, rows, 128), vmem(4, SPAN, 16, 128), vmem(SPAN, 2, 2, DEPTH, 128)],
        [smem] * 7 + [pltpu.VMEM] * 7,
        [
            vmem(2, 9 * DEPTH, 128),
            vmem(2, (width + 2) * DEPTH, 128),
            vmem(2, rows, 128),
            vmem(7, rows, 128),
            dma(8),
        ],
    )(*blocks, *sources, wave, stiff, buoy, swap_a, swap_b, *perts)

    longest = max(len(rest) for rest in NEXT)
    passed = call(
        pass_kernel, "pass_on", [vmem(ROWS, 128)] * longest, [pltpu.VMEM] * (len(FIRST) + 1), []
    )(*got[: len(FIRST)], prep)
    nexts = [
        along_rows(value, [(head, rest[n]) for head, rest in zip(FIRST, NEXT) if n < len(rest)])
        for n, value in enumerate(passed)
    ]
    operands = (*blocks, *sources, *got, *nexts, prep, fields, advanced)
    result = call(
        functools.partial(born_kernel, width, width * slabs),
        "born",
        hbm(2, 2, rows, 128),
        [smem] * 7 + [pltpu.VMEM] * (len(operands) - 8) + [pltpu.HBM],
        [vmem(ROWS, 128), vmem(SPAN, 2, 2, DEPTH + 8, 128), dma(SPAN)],
        input_output_aliases={len(operands) - 1: 0},
    )(*operands)
    return result.reshape(wavefields.shape)


def solution(mesh):
    field = P("probe", None, None, "gx", None, None)
    return jax.shard_map(
        on_device,
        mesh=mesh,
        in_specs=(field, P("gx", None, None), P("gx", None, None)) + (P(),) * 9,
        out_specs=field,
        check_vma=False,
    )
```

```python
import functools

import jax
import jax.numpy as jnp
from jax import lax
from jax.experimental import pallas as pl
from jax.experimental.pallas import tpu as pltpu
from jax.sharding import PartitionSpec as P

EDGE = 8
SPAN = EDGE + 4
DEPTH = 32
PER_ROW = 10
STRIPS = [(s, 1, i) for s in range(2) for i in range(SPAN)] + [
    (s, 0, i) for s in range(2) for i in range(1, SPAN - 1)
]
ROWS = 64

FIRST = (1, 2, 6, 8)
NEXT = ((9, 3, 7, 5), (10, 4, 12), (14, 15), (11,))
DIRECT = (13,)

PARAMS = pltpu.CompilerParams(vmem_limit_bytes=32 * 1024 * 1024)


def copy_all(pairs, sems, start=0):
    copies = [pltpu.make_async_copy(a, b, sems.at[start + n]) for n, (a, b) in enumerate(pairs)]
    for copy in copies:
        copy.start()
    return copies


def wait_all(copies):
    for copy in copies:
        copy.wait()


def wrapped(shift):
    return jnp.bitwise_and(shift + 128, 127)


def plane_rows(p, count=1):
    start = p * DEPTH
    return pl.ds(start if isinstance(p, int) else pl.multiple_of(start, DEPTH), count * DEPTH)


def at(ref, n):
    values = ref[...].reshape(1, -1)
    lane = lax.broadcasted_iota(jnp.int32, values.shape, 1)
    return jnp.sum(jnp.where(lane == n, values, jnp.zeros_like(values)))


def window(blocks, g, first):
    xb, zb, yb = (at(ref, g) for ref in blocks)
    return xb * EDGE - 2 - first, jnp.clip(zb * EDGE - 2, 0, DEPTH - SPAN), yb * EDGE - 2


def met(x0, width):
    return (x0 < width) & (x0 + SPAN > 0)


def from_sides(swap_a, swap_b, act):
    even = lax.rem(lax.axis_index("gx"), 2) == 0

    @pl.when(even)
    def _():
        act(swap_b, swap_a)

    @pl.when(jnp.logical_not(even))
    def _():
        act(swap_a, swap_b)


def edge_kernel(width, wave, stiff, buoy, swap_a, swap_b, sem):
    def pack(low, high):
        pairs = []
        for out, outer, inner in ((low, 0, 0), (high, width - 1, width - 2)):
            for s in range(2):
                pairs.append((wave.at[s, 1, plane_rows(inner, 2)], out.at[plane_rows(2 * s, 2)]))
                pairs.append((wave.at[s, 0, plane_rows(outer)], out.at[plane_rows(4 + s)]))
            pairs.append((buoy.at[plane_rows(inner, 2)], out.at[plane_rows(6, 2)]))
            pairs.append((stiff.at[plane_rows(outer)], out.at[plane_rows(8)]))
        wait_all(copy_all(pairs, sem))

    from_sides(swap_a, swap_b, pack)


def keep_sides(swap_a, swap_b, sides):
    def act(below, above):
        sides[0] = below[...]
        sides[1] = above[...]

    from_sides(swap_a, swap_b, act)


def split_kernel(width, xb, zb, yb, wave, swap_b, swap_a, *refs):
    outs, sides = refs[:-1], refs[-1]
    packs = [(head, *rest) for head, rest in zip(FIRST, NEXT)] + [(row,) for row in DIRECT]

    @pl.when(lax.axis_index("probe") == 0)
    def _():
        first = lax.axis_index("gx") * width
        keep_sides(swap_a, swap_b, sides)
        lane = lax.broadcasted_iota(jnp.int32, (8, 128), 1)

        starts = xb[...].reshape(1, -1) * EDGE - 2 - first
        each_bit = jnp.left_shift(1, lax.broadcasted_iota(jnp.int32, starts.shape, 1))
        bits = jnp.sum(jnp.where(met(starts, width), each_bit, 0))

        def cut(g, out, spot_of):

            @pl.when(jnp.bitwise_and(jnp.right_shift(bits, g), 1) == 1)
            def _():
                x0, z0, y0 = window((xb, zb, yb), g, first)

                def place(n, load):
                    k, q = divmod(n, PER_ROW)
                    for half in (0, SPAN - 8):
                        spot = pl.ds(spot_of * ROWS + k * SPAN + half, 8)
                        values = pltpu.roll(load(half), wrapped(SPAN * q - y0), 1)
                        mine = (lane >= SPAN * q) & (lane < SPAN * (q + 1))
                        out[spot, :] = jnp.where(mine, values, out[spot, :])

                for i in range(SPAN):
                    p = x0 + i
                    strips = [(n, s, t) for n, (s, t, j) in enumerate(STRIPS) if j == i]

                    @pl.when((p >= 0) & (p < width))
                    def _():
                        for n, s, t in strips:
                            place(n, lambda half: wave[s, t, pl.ds(p * DEPTH + z0 + half, 8), :])

                    @pl.when(((p >= -2) & (p < 0)) | ((p >= width) & (p < width + 2)))
                    def _():
                        side = jnp.where(p < 0, 0, 1)
                        j = jnp.where(p < 0, p + 2, p - width)
                        for n, s, t in strips:
                            top = (2 * s + j if t else 4 + s) * DEPTH + z0
                            place(n, lambda half: sides[side, pl.ds(top + half, 8), :])

        for out, members in zip(outs, packs):

            def each(n, carry):
                row = jnp.int32(members[0])
                for m, member in enumerate(members[1:], 1):
                    row = jnp.where(n == m, member, row)
                cut(row - 1, out, n)
                return carry

            lax.fori_loop(0, len(members), each, 0)


def pass_kernel(*refs):
    got, outs = refs[: len(FIRST)], refs[len(FIRST) + 1 :]
    row = lax.axis_index("probe")
    for head, rest, source in zip(FIRST, NEXT, got):

        @pl.when(row == head)
        def _():
            for n, out in zip(range(len(rest)), outs):
                out[...] = source[pl.ds((1 + n) * ROWS, ROWS), :]


def march_kernel(width, rows_of, *refs):
    @pl.when(rows_of(lax.axis_index("probe")))
    def _():
        march(width, *refs[:14], *refs[-8:])


def march(
    width, xb, zb, yb, sx, sz, sy, wavelet, wave, stiff, buoy, swap_b, swap_a, pstiff, pbuoy, out, prep, fields,
    sides, mid, later, weights, sem_out,
):
    first = lax.axis_index("gx") * width
    row = lax.axis_index("probe")
    keep_sides(swap_a, swap_b, sides)
    lane = lax.broadcasted_iota(jnp.int32, (DEPTH, 128), 1)
    depth = lax.broadcasted_iota(jnp.int32, (DEPTH, 128), 0)
    top, bottom = depth == 0, depth == DEPTH - 1
    left, right = lane == 0, lane == 127

    def present(s, p):
        if isinstance(p, int) and p < 0:
            return sides[0, plane_rows(2 * s + p + 2), :]
        if isinstance(p, int) and p >= width:
            return sides[1, plane_rows(2 * s + p - width), :]
        return wave[s, 1, plane_rows(p), :]

    def earlier(s, p):
        if isinstance(p, int) and (p < 0 or p >= width):
            return sides[0 if p < 0 else 1, plane_rows(4 + s), :]
        return wave[s, 0, plane_rows(p), :]

    def coefficients(p):
        if isinstance(p, int) and (p < 0 or p >= width):
            side = 0 if p < 0 else 1
            return sides[side, plane_rows(6 + (p + 2 if p < 0 else p - width)), :], sides[side, plane_rows(8), :]
        return buoy[plane_rows(p), :], stiff[plane_rows(p), :]

    def weigh(c, cxm, cxp, czm, czp, k):
        k = 0.5 * k
        edge = k * c
        wide = [k * (c + cxm), k * (c + cxp)]
        total = wide[0] + wide[1]
        for value, outside in (
            (czm, top),
            (czp, bottom),
            (pltpu.roll(c, 1, 1), left),
            (pltpu.roll(c, 127, 1), right),
        ):
            full = k * (c + value)
            total += jnp.where(outside, edge, full)
            wide.append(jnp.where(outside, 0.0, full))
        return wide + [2.0 - total]

    def weighted(w, v, vxm, vxp, vzm, vzp, before):
        near = (w[0] * vxm + w[1] * vxp) + (w[2] * vzm + w[3] * vzp)
        near += w[4] * pltpu.roll(v, 1, 1) + w[5] * pltpu.roll(v, 127, 1)
        return (w[6] * v - before) + near

    def save(w, p):
        for n in range(7):
            weights[n, plane_rows(p), :] = w[n]

    def up(v):
        return pltpu.roll(v, 1, 0)

    def down(v):
        return pltpu.roll(v, DEPTH - 1, 0)

    for p in (-1, 0, width - 1, width):
        c, k = coefficients(p)
        w = weigh(c, coefficients(p - 1)[0], coefficients(p + 1)[0], up(c), down(c), k)
        if 0 <= p < width:
            save(w, p)
        for s in range(2):
            v = present(s, p)
            mid[s, plane_rows(p + 1), :] = weighted(
                w, v, present(s, p - 1), present(s, p + 1), up(v), down(v), earlier(s, p)
            )

    def step_one(p, carry):
        above, below = pl.ds(p * DEPTH - 1, DEPTH), pl.ds(p * DEPTH + 1, DEPTH)
        c, k = coefficients(p)
        w = weigh(c, buoy[plane_rows(p - 1), :], buoy[plane_rows(p + 1), :], buoy[above, :], buoy[below, :], k)
        save(w, p)
        for s in range(2):
            mid[s, plane_rows(p + 1), :] = weighted(
                w, present(s, p), present(s, p - 1), present(s, p + 1), wave[s, 1, above, :], wave[s, 1, below, :],
                earlier(s, p),
            )
        return carry

    lax.fori_loop(1, width - 1, step_one, 0, unroll=width - 2)

    def inject(ref, step, low, high, shift):
        for s in range(2):
            @pl.when(row == 0)
            def _():
                x = at(sx, s) - first

                @pl.when((x >= low) & (x < high))
                def _():
                    hit = (lane == at(sy, s)) & (depth == at(sz, s))
                    spot = plane_rows(x + shift)
                    ref[s, spot, :] = ref[s, spot, :] + jnp.where(hit, at(wavelet.at[s], step), 0.0)

    inject(mid, 0, -1, width + 1, 1)
    outs = copy_all([(mid.at[s, plane_rows(1, width)], out.at[s, 0]) for s in range(2)], sem_out)

    def step_two(p, carry):
        above, below = pl.ds((p + 1) * DEPTH - 1, DEPTH), pl.ds((p + 1) * DEPTH + 1, DEPTH)
        w = [weights[n, plane_rows(p), :] for n in range(7)]
        for s in range(2):
            later[s, plane_rows(p), :] = weighted(
                w, mid[s, plane_rows(p + 1), :], mid[s, plane_rows(p), :], mid[s, plane_rows(p + 2), :],
                mid[s, above, :], mid[s, below, :], present(s, p),
            )
        return carry

    part = width // 3
    for n in range(3):
        low, high = n * part, (n + 1) * part
        lax.fori_loop(low, high, step_two, 0, unroll=part)
        inject(later, 1, low, high, 0)
        pairs = [(later.at[s, plane_rows(low, part)], out.at[s, 1, plane_rows(low, part)]) for s in range(2)]
        outs += copy_all(pairs, sem_out, 2 + 2 * n)

    g = jnp.maximum(row - 1, 0)
    x0, z0, y0 = window((xb, zb, yb), g, first)

    @pl.when((row > 0) & met(x0, width))
    def _():
        strip = lax.broadcasted_iota(jnp.int32, (8, 128), 1)
        here = (strip < SPAN) & (strip + y0 >= 0) & (strip + y0 < 128)
        prep[...] = jnp.zeros(prep.shape, jnp.float32)

        def bring(n, i, load):
            for half in (0, SPAN - 8):
                prep[n, i, pl.ds(half, 8), :] = jnp.where(here, pltpu.roll(load(half), wrapped(-y0), 1), 0.0)

        for i in range(SPAN):
            p = x0 + i

            @pl.when((p >= 0) & (p < width))
            def _():
                bring(0, i, lambda half: buoy[pl.ds(p * DEPTH + z0 + half, 8), :])
                bring(1, i, lambda half: stiff[pl.ds(p * DEPTH + z0 + half, 8), :])
                for s in range(2):
                    fields[i, s, 0] = mid[s, plane_rows(p + 1), :]
                    fields[i, s, 1] = later[s, plane_rows(p), :]

            side = jnp.where(p < 0, 0, 1)
            j = jnp.where(p < 0, p + 2, p - width)

            @pl.when(((p >= -2) & (p < 0)) | ((p >= width) & (p < width + 2)))
            def _():
                bring(0, i, lambda half: sides[side, pl.ds((6 + j) * DEPTH + z0 + half, 8), :])

            @pl.when((p == -1) | (p == width))
            def _():
                bring(1, i, lambda half: sides[side, pl.ds(8 * DEPTH + z0 + half, 8), :])

        wide = lax.broadcasted_iota(jnp.int32, (EDGE, EDGE, pstiff.shape[-1]), 2)
        diagonal = lax.broadcasted_iota(jnp.int32, (EDGE, EDGE, 128), 2)
        diagonal = diagonal == lax.broadcasted_iota(jnp.int32, (EDGE, EDGE, 128), 1) + 2
        dz = at(zb, g) * EDGE - z0
        for n, ref in ((2, pstiff), (3, pbuoy)):
            for i in range(EDGE):
                column = jnp.sum(jnp.where(wide == g, ref[i], 0.0), axis=2, keepdims=True)
                prep[n, 2 + i, pl.ds(dz, EDGE), :] = jnp.sum(jnp.where(diagonal, column, 0.0), axis=1)

    wait_all(outs)


def born_kernel(width, extent, xb, zb, yb, sx, sz, sy, wavelet, *refs):
    count = len(FIRST) + len(DIRECT)
    longest = max(len(rest) for rest in NEXT)
    firsts, directs, nexts = refs[: len(FIRST)], refs[len(FIRST) : count], refs[count : count + longest]
    prep, fields, _, out, piece, planes, sem = refs[count + longest :]
    row = lax.axis_index("probe")
    g = jnp.maximum(row - 1, 0)
    first = lax.axis_index("gx") * width
    x0, z0, y0 = window((xb, zb, yb), g, first)

    @pl.when((row > 0) & met(x0, width))
    def _():
        def bring(where, source):
            @pl.when(where)
            def _():
                piece[...] = source[pl.ds(0, ROWS), :]

        for target, source in zip(FIRST + DIRECT, (*firsts, *directs)):
            bring(row == target, source)
        for n, source in enumerate(nexts):
            where = row < 0
            for rest in NEXT:
                if n < len(rest):
                    where = where | (row == rest[n])
            bring(where, source)

        lane = lax.broadcasted_iota(jnp.int32, (16, 128), 1)
        depth = lax.broadcasted_iota(jnp.int32, (16, 128), 0)
        here = (lane < SPAN) & (depth < SPAN) & (lane + y0 >= 0) & (lane + y0 < 128)
        c, k, sb, bb = (prep[n] for n in range(4))

        def field(s, t):
            got = []
            for i in range(SPAN):
                if (s, t, i) not in STRIPS:
                    got.append(jnp.zeros((16, 128), jnp.float32))
                    continue
                n, q = divmod(STRIPS.index((s, t, i)), PER_ROW)
                values = piece[pl.ds(n * SPAN, 16), :]
                if q:
                    values = pltpu.roll(values, 128 - SPAN * q, 1)
                x = x0 + i
                ok = (first + x >= 0) & (first + x < extent) & (x >= -1 - t) & (x < width + 1 + t)
                got.append(jnp.where(here & ok, values, 0.0))
            return jnp.stack(got)

        def up(v, axis):
            return pltpu.roll(v, v.shape[axis] - 1, axis)

        def faces(coef):
            return 0.5 * (coef[1:] + coef[:-1]), 0.5 * (coef + up(coef, 1)), 0.5 * (coef + up(coef, 2))

        def steps(v):
            return v[1:] - v[:-1], up(v, 1) - v, up(v, 2) - v

        def gather(coef, step):
            fx, fz, fy = (a * b for a, b in zip(coef, step))
            zero = jnp.zeros((1, 16, 128), jnp.float32)
            total = jnp.concatenate([fx, zero], 0) - jnp.concatenate([zero, fx], 0)
            total += fz - pltpu.roll(fz, 1, 1)
            total += fy - pltpu.roll(fy, 1, 2)
            return total

        of_c = faces(c)
        of_b = faces(bb)
        for s in range(2):
            now = field(s, 1)
            step = steps(now)
            laplace = gather(of_c, step)
            forcing = sb * laplace + k * gather(of_b, step)
            hit = here & (lane + y0 == at(sy, s)) & (depth + z0 == at(sz, s))
            x, amplitude = at(sx, s), at(wavelet.at[s], 0)
            source = []
            for i in range(SPAN):
                source.append(jnp.where(hit & (first + x0 + i == x), amplitude, 0.0))
            then = steps(2.0 * now - field(s, 0) + k * laplace + jnp.stack(source))
            second = sb * gather(of_c, then) + k * gather(of_b, then)
            gains = (forcing, 2.0 * forcing + k * gather(of_c, steps(forcing)) + second)
            for t in range(2):
                moved = pltpu.roll(gains[t], wrapped(y0), 2)
                for i in range(SPAN):
                    planes[i, s, t, pl.ds(0, DEPTH), :] = fields[i, s, t]
                    spot = pl.ds(z0, 16)
                    planes[i, s, t, spot, :] = planes[i, s, t, spot, :] + moved[i]

        def each_plane(act):
            for i in range(SPAN):

                @pl.when((x0 + i >= 0) & (x0 + i < width))
                def _():
                    target = out.at[:, :, plane_rows(x0 + i)]
                    act(pltpu.make_async_copy(planes.at[i, :, :, pl.ds(0, DEPTH)], target, sem.at[i]))

        each_plane(lambda copy: copy.start())
        each_plane(lambda copy: copy.wait())


def on_device(
    wavefields, stiffness, buoyancy, pert_stiffness, pert_buoyancy, xblock_index, zblock_index, yblock_index,
    source_xcell, source_zcell, source_ycell, wavelet
):
    width = wavefields.shape[3]
    slabs = lax.axis_size("gx")
    rows = width * DEPTH
    wave = wavefields.reshape(2, 2, rows, 128)
    stiff, buoy = stiffness.reshape(rows, 128), buoyancy.reshape(rows, 128)
    blocks = (xblock_index, zblock_index, yblock_index)
    sources = (source_xcell, source_zcell, source_ycell, wavelet)
    perts = [jnp.transpose(p, (1, 2, 3, 0)) for p in (pert_stiffness, pert_buoyancy)]
    hbm = lambda *shape: pltpu.HBM(shape, jnp.float32)
    vmem = lambda *shape: pltpu.VMEM(shape, jnp.float32)
    dma = lambda *shape: pltpu.SemaphoreType.DMA(shape)

    def call(kernel, name, out_shape, spaces, scratch, **more):
        made = pl.pallas_call(
            kernel,
            out_shape=out_shape,
            in_specs=[pl.BlockSpec(memory_space=space) for space in spaces],
            out_specs=jax.tree.map(lambda s: pl.BlockSpec(memory_space=s.memory_space), out_shape),
            scratch_shapes=scratch,
            compiler_params=PARAMS,
            name=name,
            **more,
        )
        return lambda *args: made(*map(pltpu.with_memory_space_constraint, args, spaces))

    def along_rows(value, pairs):
        every = [(a * slabs + s, b * slabs + s) for a, b in pairs for s in range(slabs)]
        return lax.ppermute(value, ("probe", "gx"), every)

    def swap(value, start):
        pairs = [(s, s + 1) for s in range(start, slabs - 1, 2)]
        return lax.ppermute(value, "gx", pairs + [(b, a) for a, b in pairs])

    edge = vmem(9 * DEPTH, 128)
    edge_a, edge_b = call(
        functools.partial(edge_kernel, width), "edges", [edge, edge], [pltpu.HBM] * 3, [dma(12)]
    )(wave, stiff, buoy)
    swap_a, swap_b = swap(edge_a, 0), swap(edge_b, 1)

    counts = [1 + len(rest) for rest in NEXT] + [1] * len(DIRECT)
    packs = call(
        functools.partial(split_kernel, width),
        "split",
        [vmem(n * ROWS, 128) for n in counts],
        [pltpu.VMEM] * 6,
        [vmem(2, 9 * DEPTH, 128)],
    )(*blocks, wave, swap_b, swap_a)
    got = [along_rows(p, [(0, row)]) for p, row in zip(packs, FIRST + DIRECT)]

    def march_on(name, rows_of, before=()):
        marched = [hbm(2, 2, rows, 128), vmem(4, SPAN, 16, 128), vmem(SPAN, 2, 2, DEPTH, 128)]
        operands = (*blocks, *sources, wave, stiff, buoy, swap_b, swap_a, *perts, *before)
        return call(
            functools.partial(march_kernel, width, rows_of),
            name,
            marched,
            [pltpu.VMEM] * 14 + [pltpu.HBM, pltpu.VMEM, pltpu.VMEM, pltpu.VMEM][: len(before)],
            [
                vmem(2, 9 * DEPTH, 128),
                vmem(2, (width + 2) * DEPTH, 128),
                vmem(2, rows, 128),
                vmem(7, rows, 128),
                dma(8),
            ],
            input_output_aliases={14: 0, 15: 1, 16: 2} if before else {},
        )(*operands)

    late = lambda row: functools.reduce(jnp.logical_or, [row == r for r in FIRST[1:]])
    marched = march_on("march_first", late)

    longest = max(len(rest) for rest in NEXT)
    passed = call(
        pass_kernel, "pass_on", [vmem(ROWS, 128)] * longest, [pltpu.VMEM] * (len(FIRST) + 1), []
    )(*got[: len(FIRST)], marched[1])
    nexts = [
        along_rows(value, [(head, rest[n]) for head, rest in zip(FIRST, NEXT) if n < len(rest)])
        for n, value in enumerate(passed)
    ]
    advanced, prep, fields = march_on("march_rest", lambda row: jnp.logical_not(late(row)), (*marched, passed[-1]))
    operands = (*blocks, *sources, *got, *nexts, prep, fields, advanced)
    result = call(
        functools.partial(born_kernel, width, width * slabs),
        "born",
        hbm(2, 2, rows, 128),
        [pltpu.VMEM] * (len(operands) - 1) + [pltpu.HBM],
        [vmem(ROWS, 128), vmem(SPAN, 2, 2, DEPTH + 8, 128), dma(SPAN)],
        input_output_aliases={len(operands) - 1: 0},
    )(*operands)
    return result.reshape(wavefields.shape)


def solution(mesh):
    field = P("probe", None, None, "gx", None, None)
    return jax.shard_map(
        on_device,
        mesh=mesh,
        in_specs=(field, P("gx", None, None), P("gx", None, None)) + (P(),) * 9,
        out_specs=field,
        check_vma=False,
    )
```

```python
import functools

import jax
import jax.numpy as jnp
from jax import lax
from jax.experimental import pallas as pl
from jax.experimental.pallas import tpu as pltpu
from jax.sharding import PartitionSpec as P

EDGE = 8
SPAN = EDGE + 4
DEPTH = 32
GRID = 24
ROWS = 4 * SPAN


def strips_of_a_piece():
    found = []
    for n, (s, i) in enumerate((s, i) for s in range(2) for i in range(SPAN)):
        found.append((s, 1, i, n // 10 * SPAN, n % 10 * SPAN, 0, SPAN))
    for n, (s, i) in enumerate((s, i) for s in range(2) for i in range(1, SPAN - 1)):
        row, lane = (2 * SPAN, 48 + 10 * n) if n < 8 else (3 * SPAN, 10 * (n - 8))
        found.append((s, 0, i, row, lane, 1, 10))
    return found


STRIPS = strips_of_a_piece()

FIRST = (1, 2, 6, 8)
NEXT = ((9, 3, 7, 5), (10, 4, 12), (14, 15), (11,))
DIRECT = (13,)

PARAMS = pltpu.CompilerParams(vmem_limit_bytes=32 * 1024 * 1024)


def copy_all(pairs, sems, start=0):
    copies = [pltpu.make_async_copy(a, b, sems.at[start + n]) for n, (a, b) in enumerate(pairs)]
    for copy in copies:
        copy.start()
    return copies


def wait_all(copies):
    for copy in copies:
        copy.wait()


def wrapped(shift):
    return jnp.bitwise_and(shift + 128, 127)


def plane_rows(p, count=1):
    start = p * DEPTH
    return pl.ds(start if isinstance(p, int) else pl.multiple_of(start, DEPTH), count * DEPTH)


def at(ref, n):
    values = ref[...].reshape(1, -1)
    lane = lax.broadcasted_iota(jnp.int32, values.shape, 1)
    return jnp.sum(jnp.where(lane == n, values, jnp.zeros_like(values)))


def window(blocks, g, first):
    xb, zb, yb = (at(ref, g) for ref in blocks)
    return xb * EDGE - 2 - first, jnp.clip(zb * EDGE - 2, 0, DEPTH - SPAN), yb * EDGE - 2


def met(x0, width):
    return (x0 < width) & (x0 + SPAN > 0)


def swap_pairs(rows, slabs):
    rounds = [[], [], []]
    for row in range(rows):
        for low in range(slabs - 1):
            if row == 0 and low < 3:
                rounds[(1, 0, 2)[low]].append((row, low))
            else:
                rounds[low % 2].append((row, low))
    return rounds


def from_sides(swaps, act):
    slab, background = lax.axis_index("gx"), lax.axis_index("probe") == 0
    apart = background & ((slab == 2) | (slab == 3))
    turned = background & (slab < 2)
    even = (lax.rem(slab, 2) == 0) != turned
    for where, below, above in (
        (even & jnp.logical_not(apart), 1, 0),
        (jnp.logical_not(even | apart), 0, 1),
        (background & (slab == 2), 0, 2),
        (background & (slab == 3), 2, 1),
    ):

        @pl.when(where)
        def _():
            act(swaps[below], swaps[above])


def edge_kernel(width, wave, stiff, buoy, swap_a, swap_b, swap_c, sem):
    def pack(low, high):
        pairs = []
        for out, outer, inner in ((low, 0, 0), (high, width - 1, width - 2)):
            pairs.append((wave.at[:, 1, pl.ds(inner, 2)], out.at[pl.ds(0, 2), pl.ds(0, 2)]))
            pairs.append((wave.at[:, 0, outer], out.at[pl.ds(0, 2), 2]))
            pairs.append((buoy.at[pl.ds(inner, 2)], out.at[2, pl.ds(0, 2)]))
            pairs.append((stiff.at[outer], out.at[2, 2]))
        wait_all(copy_all(pairs, sem))

    from_sides((swap_a, swap_b, swap_c), pack)


def keep_sides(swaps, sides):
    def act(below, above):
        sides[0] = below[...]
        sides[1] = above[...]

    from_sides(swaps, act)


def split_kernel(width, xb, zb, yb, wave, swap_b, swap_a, swap_c, *refs):
    *outs, sides, near = refs
    packs = [(head, *rest) for head, rest in zip(FIRST, NEXT)] + [(row,) for row in DIRECT]

    @pl.when(lax.axis_index("probe") == 0)
    def _():
        first = lax.axis_index("gx") * width
        keep_sides((swap_a, swap_b, swap_c), sides)
        lane = lax.broadcasted_iota(jnp.int32, (16, 128), 1)
        starts = xb[...].reshape(1, -1) * EDGE - 2 - first
        each_bit = jnp.left_shift(1, lax.broadcasted_iota(jnp.int32, starts.shape, 1))
        bits = jnp.sum(jnp.where(met(starts, width), each_bit, 0))

        def cut(g, out, n):
            @pl.when(jnp.bitwise_and(jnp.right_shift(bits, g), 1) == 1)
            def _():
                x0, z0, y0 = window((xb, zb, yb), g, first)
                for i in range(SPAN):
                    p = x0 + i

                    @pl.when((p >= 0) & (p < width))
                    def _():
                        for s, t in ((0, 0), (0, 1), (1, 0), (1, 1)):
                            for half in (0, SPAN - 8):
                                near[s, t, i, pl.ds(half, 8), :] = wave[s, t, pl.ds(p * DEPTH + z0 + half, 8), :]

                    @pl.when(((p >= -2) & (p < 0)) | ((p >= width) & (p < width + 2)))
                    def _():
                        side = jnp.where(p < 0, 0, 1)
                        j = jnp.where(p < 0, p + 2, p - width)
                        for s, t in ((0, 0), (0, 1), (1, 0), (1, 1)):
                            top = (3 * s + (j if t else 2)) * DEPTH + z0
                            for half in (0, SPAN - 8):
                                near[s, t, i, pl.ds(half, 8), :] = sides[side, pl.ds(top + half, 8), :]

                for row in range(0, ROWS, SPAN):
                    packed = jnp.zeros((16, 128), jnp.float32)
                    for s, t, i, _, start, y, count in (strip for strip in STRIPS if strip[3] == row):
                        values = pltpu.roll(near[s, t, i], wrapped(start - y - y0), 1)
                        packed = jnp.where((lane >= start) & (lane < start + count), values, packed)
                    spot = n * ROWS + row
                    out[pl.ds(spot, 8), :] = packed[:8]
                    out[pl.ds(spot + 8, SPAN - 8), :] = packed[8:SPAN]

        for out, members in zip(outs, packs):

            def each(n, carry):
                row = jnp.int32(members[0])
                for m, member in enumerate(members[1:], 1):
                    row = jnp.where(n == m, member, row)
                cut(row - 1, out, n)
                return carry

            lax.fori_loop(0, len(members), each, 0)


def pass_kernel(*refs):
    got, outs = refs[: len(FIRST)], refs[len(FIRST) + 1 :]
    row = lax.axis_index("probe")
    for head, rest, source in zip(FIRST, NEXT, got):

        @pl.when(row == head)
        def _():
            for n, out in zip(range(len(rest)), outs):
                out[...] = source[pl.ds((1 + n) * ROWS, ROWS), :]


def march_kernel(width, rows_of, *refs):
    @pl.when(rows_of(lax.axis_index("probe")))
    def _():
        march(width, *refs[:15], *refs[-9:])


def march(
    width, xb, zb, yb, sx, sz, sy, wavelet, wave, stiff, buoy, swap_b, swap_a, swap_c, pstiff, pbuoy, out, prep, fields,
    sides, mid, later, weights, near, sem_out,
):
    first = lax.axis_index("gx") * width
    row = lax.axis_index("probe")
    keep_sides((swap_a, swap_b, swap_c), sides)
    lane = lax.broadcasted_iota(jnp.int32, (DEPTH, 128), 1)
    depth = lax.broadcasted_iota(jnp.int32, (DEPTH, 128), 0)
    top, bottom = depth == 0, depth == DEPTH - 1
    left, right = lane == 0, lane == 127

    def present(s, p):
        if isinstance(p, int) and p < 0:
            return sides[0, plane_rows(3 * s + p + 2), :]
        if isinstance(p, int) and p >= width:
            return sides[1, plane_rows(3 * s + p - width), :]
        return wave[s, 1, plane_rows(p), :]

    def earlier(s, p):
        if isinstance(p, int) and (p < 0 or p >= width):
            return sides[0 if p < 0 else 1, plane_rows(3 * s + 2), :]
        return wave[s, 0, plane_rows(p), :]

    def coefficients(p):
        if isinstance(p, int) and (p < 0 or p >= width):
            side = 0 if p < 0 else 1
            return sides[side, plane_rows(6 + (p + 2 if p < 0 else p - width)), :], sides[side, plane_rows(8), :]
        return buoy[plane_rows(p), :], stiff[plane_rows(p), :]

    def weigh(c, cxm, cxp, czm, czp, k):
        k = 0.5 * k
        edge = k * c
        wide = [k * (c + cxm), k * (c + cxp)]
        total = wide[0] + wide[1]
        for value, outside in (
            (czm, top),
            (czp, bottom),
            (pltpu.roll(c, 1, 1), left),
            (pltpu.roll(c, 127, 1), right),
        ):
            full = k * (c + value)
            total += jnp.where(outside, edge, full)
            wide.append(jnp.where(outside, 0.0, full))
        return wide + [2.0 - total]

    def weighted(w, v, vxm, vxp, vzm, vzp, before):
        near = (w[0] * vxm + w[1] * vxp) + (w[2] * vzm + w[3] * vzp)
        near += w[4] * pltpu.roll(v, 1, 1) + w[5] * pltpu.roll(v, 127, 1)
        return (w[6] * v - before) + near

    def save(w, p):
        for n in range(7):
            weights[n, plane_rows(p), :] = w[n]

    def up(v):
        return pltpu.roll(v, 1, 0)

    def down(v):
        return pltpu.roll(v, DEPTH - 1, 0)

    for p in (-1, 0, width - 1, width):
        c, k = coefficients(p)
        w = weigh(c, coefficients(p - 1)[0], coefficients(p + 1)[0], up(c), down(c), k)
        if 0 <= p < width:
            save(w, p)
        for s in range(2):
            v = present(s, p)
            mid[s, plane_rows(p + 1), :] = weighted(
                w, v, present(s, p - 1), present(s, p + 1), up(v), down(v), earlier(s, p)
            )

    def step_one(p, carry):
        above, below = pl.ds(p * DEPTH - 1, DEPTH), pl.ds(p * DEPTH + 1, DEPTH)
        c, k = coefficients(p)
        w = weigh(c, buoy[plane_rows(p - 1), :], buoy[plane_rows(p + 1), :], buoy[above, :], buoy[below, :], k)
        save(w, p)
        for s in range(2):
            mid[s, plane_rows(p + 1), :] = weighted(
                w, present(s, p), present(s, p - 1), present(s, p + 1), wave[s, 1, above, :], wave[s, 1, below, :],
                earlier(s, p),
            )
        return carry

    lax.fori_loop(1, width - 1, step_one, 0, unroll=width - 2)

    sources = [at(sx, s) - first for s in range(2)]

    def inject(ref, step, low, high, shift):
        for s, x in enumerate(sources):

            @pl.when((row == 0) & (x >= low) & (x < high))
            def _():
                hit = (lane == at(sy, s)) & (depth == at(sz, s))
                spot = plane_rows(x + shift)
                ref[s, spot, :] = ref[s, spot, :] + jnp.where(hit, at(wavelet.at[s], step), 0.0)

    inject(mid, 0, -1, width + 1, 1)
    outs = copy_all([(mid.at[s, plane_rows(1, width)], out.at[s, 0]) for s in range(2)], sem_out)

    def step_two(p, carry):
        above, below = pl.ds((p + 1) * DEPTH - 1, DEPTH), pl.ds((p + 1) * DEPTH + 1, DEPTH)
        w = [weights[n, plane_rows(p), :] for n in range(7)]
        for s in range(2):
            later[s, plane_rows(p), :] = weighted(
                w, mid[s, plane_rows(p + 1), :], mid[s, plane_rows(p), :], mid[s, plane_rows(p + 2), :],
                mid[s, above, :], mid[s, below, :], present(s, p),
            )
        return carry

    part = width // 3
    for n in range(3):
        low, high = n * part, (n + 1) * part
        lax.fori_loop(low, high, step_two, 0, unroll=part)
        inject(later, 1, low, high, 0)
        pairs = [(later.at[s, plane_rows(low, part)], out.at[s, 1, plane_rows(low, part)]) for s in range(2)]
        outs += copy_all(pairs, sem_out, 2 + 2 * n)

    g = jnp.maximum(row - 1, 0)
    x0, z0, y0 = window((xb, zb, yb), g, first)

    @pl.when((row > 0) & met(x0, width))
    def _():
        strip = lax.broadcasted_iota(jnp.int32, (8, 128), 1)
        here = (strip < SPAN) & (strip + y0 >= 0) & (strip + y0 < 128)
        near[...] = jnp.zeros(near.shape, jnp.float32)

        def bring(n, i, load):
            for half in (0, SPAN - 8):
                near[n, i, pl.ds(half, 8), :] = jnp.where(here, pltpu.roll(load(half), wrapped(-y0), 1), 0.0)

        for i in range(SPAN):
            p = x0 + i

            @pl.when((p >= 0) & (p < width))
            def _():
                bring(0, i, lambda half: buoy[pl.ds(p * DEPTH + z0 + half, 8), :])
                bring(1, i, lambda half: stiff[pl.ds(p * DEPTH + z0 + half, 8), :])
                for s in range(2):
                    fields[i, s, 0, pl.ds(0, DEPTH), :] = mid[s, plane_rows(p + 1), :]
                    fields[i, s, 1, pl.ds(0, DEPTH), :] = later[s, plane_rows(p), :]

            side = jnp.where(p < 0, 0, 1)
            j = jnp.where(p < 0, p + 2, p - width)

            @pl.when(((p >= -2) & (p < 0)) | ((p >= width) & (p < width + 2)))
            def _():
                bring(0, i, lambda half: sides[side, pl.ds((6 + j) * DEPTH + z0 + half, 8), :])

            @pl.when((p == -1) | (p == width))
            def _():
                bring(1, i, lambda half: sides[side, pl.ds(8 * DEPTH + z0 + half, 8), :])

        wide = lax.broadcasted_iota(jnp.int32, (EDGE, EDGE, pstiff.shape[-1]), 2)
        diagonal = lax.broadcasted_iota(jnp.int32, (EDGE, EDGE, 128), 2)
        diagonal = diagonal == lax.broadcasted_iota(jnp.int32, (EDGE, EDGE, 128), 1) + 2
        dz = at(zb, g) * EDGE - z0
        for n, ref in ((2, pstiff), (3, pbuoy)):
            for i in range(EDGE):
                column = jnp.sum(jnp.where(wide == g, ref[i], 0.0), axis=2, keepdims=True)
                near[n, 2 + i, pl.ds(dz, EDGE), :] = jnp.sum(jnp.where(diagonal, column, 0.0), axis=1)

        none = jnp.zeros((16, 128), jnp.float32)

        def faces(n, i):
            c = near[n, i]
            x = [0.5 * (c + near[n, i + d]) if 0 <= i + d < SPAN else none for d in (-1, 1)]
            z, y = 0.5 * (c + pltpu.roll(c, 15, 0)), 0.5 * (c + pltpu.roll(c, 127, 1))
            return [*x, pltpu.roll(z, 1, 0), z, pltpu.roll(y, 1, 1), y]

        for i in range(SPAN):
            k, sb = near[1, i], near[2, i]
            forced, free = none, 2.0 + none
            for n, (a, b) in enumerate(zip(faces(0, i), faces(3, i))):
                given, own = sb * a + k * b, k * a
                prep[n, i], prep[7 + n, i] = given, own
                forced, free = forced - given, free - own
            prep[6, i], prep[13, i] = forced, free

    wait_all(outs)


def born_kernel(width, extent, xb, zb, yb, sx, sz, sy, wavelet, *refs):
    count = len(FIRST) + len(DIRECT)
    longest = max(len(rest) for rest in NEXT)
    firsts, directs, nexts = refs[: len(FIRST)], refs[len(FIRST) : count], refs[count : count + longest]
    prep, fields, _, out, piece, planes, now, later, forced, sem = refs[count + longest :]
    row = lax.axis_index("probe")
    g = jnp.maximum(row - 1, 0)
    first = lax.axis_index("gx") * width
    x0, z0, y0 = window((xb, zb, yb), g, first)

    @pl.when((row > 0) & met(x0, width))
    def _():
        def bring(where, source):
            @pl.when(where)
            def _():
                piece[pl.ds(0, ROWS), :] = source[pl.ds(0, ROWS), :]

        for target, source in zip(FIRST + DIRECT, (*firsts, *directs)):
            bring(row == target, source)
        for n, source in enumerate(nexts):
            where = row < 0
            for rest in NEXT:
                if n < len(rest):
                    where = where | (row == rest[n])
            bring(where, source)

        planes[...] = fields[...]
        lane = lax.broadcasted_iota(jnp.int32, (16, 128), 1)
        depth = lax.broadcasted_iota(jnp.int32, (16, 128), 0)
        here = (lane < SPAN) & (depth < SPAN) & (lane + y0 >= 0) & (lane + y0 < 128)
        inner = here & (lane >= 1) & (lane < SPAN - 1)
        blank = jnp.zeros((8, 128), jnp.float32)
        for ref in (now, later, forced):
            for s in range(2):
                for i in range(SPAN + 1):
                    ref[s, pl.ds(i * GRID, 8), :] = blank

        def strip(s, t, i):
            found = [strip for strip in STRIPS if strip[:3] == (s, t, i)]
            if not found:
                return jnp.zeros((16, 128), jnp.float32)
            _, _, _, row, start, y, _ = found[0]
            values = piece[pl.ds(row, 16), :]
            if start != y:
                values = pltpu.roll(values, (y - start) % 128, 1)
            x = x0 + i
            ok = (first + x >= 0) & (first + x < extent) & (x >= -1 - t) & (x < width + 1 + t)
            return jnp.where((here if t else inner) & ok, values, 0.0)

        def cells(i, shift=0):
            return pl.ds(i * GRID + 8 + shift, 16)

        def around(ref, s, i):
            v = ref[s, cells(i), :]
            x = [ref[s, cells(i + d), :] if 0 <= i + d < SPAN else None for d in (-1, 1)]
            z = [ref[s, cells(i, d), :] for d in (-1, 1)]
            return [*x, *z, pltpu.roll(v, 1, 1), pltpu.roll(v, 127, 1), v]

        def weighted(w, values):
            terms = [a * b for a, b in zip(w, values) if b is not None]
            return functools.reduce(jnp.add, terms)

        for s in range(2):
            for i in range(SPAN):
                now[s, cells(i), :] = strip(s, 1, i)
        shots = []
        for s in range(2):
            hit = here & (lane + y0 == at(sy, s)) & (depth + z0 == at(sz, s))
            shots.append((at(sx, s) - first - x0, jnp.where(hit, at(wavelet.at[s], 0), 0.0)))
        for i in range(SPAN):
            of_forcing, of_step = ([prep[n + m, i] for n in range(7)] for m in (0, 7))
            for s, (x, source) in enumerate(shots):
                values = around(now, s, i)
                forced[s, cells(i), :] = weighted(of_forcing, values)
                after = weighted(of_step, values) - strip(s, 0, i)
                later[s, cells(i), :] = after + jnp.where(x == i, source, 0.0)

        def each_plane(act, low=0, high=SPAN):
            for i in range(low, high):

                @pl.when((x0 + i >= 0) & (x0 + i < width))
                def _():
                    target = out.at[:, :, plane_rows(x0 + i)]
                    act(pltpu.make_async_copy(planes.at[i, :, :, pl.ds(0, DEPTH)], target, sem.at[i]))

        part = SPAN // 3
        for low in range(0, SPAN, part):
            for i in range(low, low + part):
                of_forcing, of_step = ([prep[n + m, i] for n in range(7)] for m in (0, 7))
                for s in range(2):
                    gain = forced[s, cells(i), :]
                    more = weighted(of_step, around(forced, s, i)) + weighted(of_forcing, around(later, s, i))
                    for t, value in enumerate((gain, more)):
                        spot = pl.ds(z0, 16)
                        planes[i, s, t, spot, :] = fields[i, s, t, spot, :] + pltpu.roll(value, wrapped(y0), 1)
            each_plane(lambda copy: copy.start(), low, low + part)
        each_plane(lambda copy: copy.wait())


def on_device(
    wavefields, stiffness, buoyancy, pert_stiffness, pert_buoyancy, xblock_index, zblock_index, yblock_index,
    source_xcell, source_zcell, source_ycell, wavelet
):
    width = wavefields.shape[3]
    slabs = lax.axis_size("gx")
    rows = width * DEPTH
    wave = wavefields.reshape(2, 2, rows, 128)
    stiff, buoy = stiffness.reshape(rows, 128), buoyancy.reshape(rows, 128)
    blocks = (xblock_index, zblock_index, yblock_index)
    sources = (source_xcell, source_zcell, source_ycell, wavelet)
    perts = [jnp.transpose(p, (1, 2, 3, 0)) for p in (pert_stiffness, pert_buoyancy)]
    hbm = lambda *shape: pltpu.HBM(shape, jnp.float32)
    vmem = lambda *shape: pltpu.VMEM(shape, jnp.float32)
    dma = lambda *shape: pltpu.SemaphoreType.DMA(shape)

    def call(kernel, name, out_shape, spaces, scratch, **more):
        made = pl.pallas_call(
            kernel,
            out_shape=out_shape,
            in_specs=[pl.BlockSpec(memory_space=space) for space in spaces],
            out_specs=jax.tree.map(lambda s: pl.BlockSpec(memory_space=s.memory_space), out_shape),
            scratch_shapes=scratch,
            compiler_params=PARAMS,
            name=name,
            **more,
        )
        return lambda *args: made(*map(pltpu.with_memory_space_constraint, args, spaces))

    def along_rows(value, pairs):
        every = [(a * slabs + s, b * slabs + s) for a, b in pairs for s in range(slabs)]
        return lax.ppermute(value, ("probe", "gx"), every)

    def swap(value, pairs):
        both = [(row, a, b) for row, low in pairs for a, b in ((low, low + 1), (low + 1, low))]
        return lax.ppermute(value, ("probe", "gx"), [(row * slabs + a, row * slabs + b) for row, a, b in both])

    edge = vmem(3, 3, DEPTH, 128)
    edge_a, edge_b, edge_c = call(
        functools.partial(edge_kernel, width), "edges", [edge] * 3, [pltpu.HBM] * 3, [dma(8)]
    )(wavefields[0], stiffness, buoyancy)
    edge_a, edge_b, edge_c = (edges.reshape(-1, 128) for edges in (edge_a, edge_b, edge_c))
    rounds = swap_pairs(lax.axis_size("probe"), slabs)
    swaps = [swap(*each) for each in zip((edge_a, edge_b, edge_c), rounds)]

    counts = [1 + len(rest) for rest in NEXT] + [1] * len(DIRECT)
    packs = call(
        functools.partial(split_kernel, width),
        "split",
        [vmem(n * ROWS, 128) for n in counts],
        [pltpu.VMEM] * 7,
        [vmem(2, 9 * DEPTH, 128), vmem(2, 2, SPAN, 16, 128)],
    )(*blocks, wave, swaps[1], swaps[0], swaps[2])
    got = [along_rows(p, [(0, row)]) for p, row in zip(packs, FIRST + DIRECT)]

    def march_on(name, rows_of, before=()):
        marched = [hbm(2, 2, rows, 128), vmem(14, SPAN, 16, 128), vmem(SPAN, 2, 2, DEPTH + 8, 128)]
        operands = (*blocks, *sources, wave, stiff, buoy, swaps[1], swaps[0], swaps[2], *perts, *before)
        return call(
            functools.partial(march_kernel, width, rows_of),
            name,
            marched,
            [pltpu.VMEM] * 15 + [pltpu.HBM, pltpu.VMEM, pltpu.VMEM, pltpu.VMEM][: len(before)],
            [
                vmem(2, 9 * DEPTH, 128),
                vmem(2, (width + 2) * DEPTH, 128),
                vmem(2, rows, 128),
                vmem(7, rows, 128),
                vmem(4, SPAN, 16, 128),
                dma(8),
            ],
            input_output_aliases={15: 0, 16: 1, 17: 2} if before else {},
        )(*operands)

    late = lambda row: functools.reduce(jnp.logical_or, [row == r for r in FIRST])
    marched = march_on("march_first", late)

    longest = max(len(rest) for rest in NEXT)
    passed = call(
        pass_kernel, "pass_on", [vmem(ROWS, 128)] * longest, [pltpu.VMEM] * (len(FIRST) + 1), []
    )(*got[: len(FIRST)], marched[1])
    nexts = [
        along_rows(value, [(head, rest[n]) for head, rest in zip(FIRST, NEXT) if n < len(rest)])
        for n, value in enumerate(passed)
    ]
    advanced, prep, fields = march_on("march_rest", lambda row: jnp.logical_not(late(row)), (*marched, passed[-1]))
    operands = (*blocks, *sources, *got, *nexts, prep, fields, advanced)
    result = call(
        functools.partial(born_kernel, width, width * slabs),
        "born",
        hbm(2, 2, rows, 128),
        [pltpu.VMEM] * (len(operands) - 1) + [pltpu.HBM],
        [
            vmem(ROWS + 8, 128),
            vmem(SPAN, 2, 2, DEPTH + 8, 128),
            *[vmem(2, SPAN * GRID + 8, 128)] * 3,
            dma(SPAN),
        ],
        input_output_aliases={len(operands) - 1: 0},
    )(*operands)
    return result.reshape(wavefields.shape)


def solution(mesh):
    field = P("probe", None, None, "gx", None, None)
    return jax.shard_map(
        on_device,
        mesh=mesh,
        in_specs=(field, P("gx", None, None), P("gx", None, None)) + (P(),) * 9,
        out_specs=field,
        check_vma=False,
    )
```

```python
import functools

import jax
import jax.numpy as jnp
from jax import lax
from jax.experimental import pallas as pl
from jax.experimental.pallas import tpu as pltpu
from jax.sharding import PartitionSpec as P

EDGE = 8
SPAN = EDGE + 4
DEPTH = 32
GRID = 24
ROWS = 4 * SPAN


def strips_of_a_piece():
    found = []
    for n, (s, i) in enumerate((s, i) for s in range(2) for i in range(SPAN)):
        found.append((s, 1, i, n // 10 * SPAN, n % 10 * SPAN, 0, SPAN))
    for n, (s, i) in enumerate((s, i) for s in range(2) for i in range(1, SPAN - 1)):
        row, lane = (2 * SPAN, 48 + 10 * n) if n < 8 else (3 * SPAN, 10 * (n - 8))
        found.append((s, 0, i, row, lane, 1, 10))
    return found


STRIPS = strips_of_a_piece()

FIRST = (1, 2, 6, 8)
NEXT = ((9, 3, 7, 5), (10, 4, 12), (14, 15), (11,))
DIRECT = (13,)

PARAMS = pltpu.CompilerParams(vmem_limit_bytes=32 * 1024 * 1024)


def copy_all(pairs, sems, start=0):
    copies = [pltpu.make_async_copy(a, b, sems.at[start + n]) for n, (a, b) in enumerate(pairs)]
    for copy in copies:
        copy.start()
    return copies


def wait_all(copies):
    for copy in copies:
        copy.wait()


def wrapped(shift):
    return jnp.bitwise_and(shift + 128, 127)


def plane_rows(p, count=1):
    start = p * DEPTH
    return pl.ds(start if isinstance(p, int) else pl.multiple_of(start, DEPTH), count * DEPTH)


def at(ref, n):
    values = ref[...].reshape(1, -1)
    lane = lax.broadcasted_iota(jnp.int32, values.shape, 1)
    return jnp.sum(jnp.where(lane == n, values, jnp.zeros_like(values)))


def window(blocks, g, first):
    xb, zb, yb = (at(ref, g) for ref in blocks)
    return xb * EDGE - 2 - first, jnp.clip(zb * EDGE - 2, 0, DEPTH - SPAN), yb * EDGE - 2


def met(x0, width):
    return (x0 < width) & (x0 + SPAN > 0)


def swap_pairs(rows, slabs):
    rounds = [[], [], []]
    for row in range(rows):
        for low in range(slabs - 1):
            if row == 0 and low < 3:
                rounds[(1, 0, 2)[low]].append((row, low))
            else:
                rounds[low % 2].append((row, low))
    return rounds


def from_sides(swaps, act):
    slab, background = lax.axis_index("gx"), lax.axis_index("probe") == 0
    apart = background & ((slab == 2) | (slab == 3))
    turned = background & (slab < 2)
    even = (lax.rem(slab, 2) == 0) != turned
    for where, below, above in (
        (even & jnp.logical_not(apart), 1, 0),
        (jnp.logical_not(even | apart), 0, 1),
        (background & (slab == 2), 0, 2),
        (background & (slab == 3), 2, 1),
    ):

        @pl.when(where)
        def _():
            act(swaps[below], swaps[above])


def edge_kernel(width, wave, stiff, buoy, swap_a, swap_b, swap_c, sem):
    def pack(low, high):
        pairs = []
        for out, outer, inner in ((low, 0, 0), (high, width - 1, width - 2)):
            pairs.append((wave.at[:, 1, pl.ds(inner, 2)], out.at[pl.ds(0, 2), pl.ds(0, 2)]))
            pairs.append((wave.at[:, 0, outer], out.at[pl.ds(0, 2), 2]))
            pairs.append((buoy.at[pl.ds(inner, 2)], out.at[2, pl.ds(0, 2)]))
            pairs.append((stiff.at[outer], out.at[2, 2]))
        wait_all(copy_all(pairs, sem))

    from_sides((swap_a, swap_b, swap_c), pack)


def keep_sides(swaps, sides):
    def act(below, above):
        sides[0] = below[...]
        sides[1] = above[...]

    from_sides(swaps, act)


def split_kernel(width, xb, zb, yb, wave, swap_b, swap_a, swap_c, *refs):
    *outs, sides, near = refs
    packs = [(head, *rest) for head, rest in zip(FIRST, NEXT)] + [(row,) for row in DIRECT]

    @pl.when(lax.axis_index("probe") == 0)
    def _():
        first = lax.axis_index("gx") * width
        keep_sides((swap_a, swap_b, swap_c), sides)
        lane = lax.broadcasted_iota(jnp.int32, (16, 128), 1)
        starts = xb[...].reshape(1, -1) * EDGE - 2 - first
        each_bit = jnp.left_shift(1, lax.broadcasted_iota(jnp.int32, starts.shape, 1))
        bits = jnp.sum(jnp.where(met(starts, width), each_bit, 0))

        def cut(g, out, n):
            @pl.when(jnp.bitwise_and(jnp.right_shift(bits, g), 1) == 1)
            def _():
                x0, z0, y0 = window((xb, zb, yb), g, first)
                for i in range(SPAN):
                    p = x0 + i

                    @pl.when((p >= 0) & (p < width))
                    def _():
                        for s, t in ((0, 0), (0, 1), (1, 0), (1, 1)):
                            for half in (0, SPAN - 8):
                                near[s, t, i, pl.ds(half, 8), :] = wave[s, t, pl.ds(p * DEPTH + z0 + half, 8), :]

                    @pl.when(((p >= -2) & (p < 0)) | ((p >= width) & (p < width + 2)))
                    def _():
                        side = jnp.where(p < 0, 0, 1)
                        j = jnp.where(p < 0, p + 2, p - width)
                        for s, t in ((0, 0), (0, 1), (1, 0), (1, 1)):
                            top = (3 * s + (j if t else 2)) * DEPTH + z0
                            for half in (0, SPAN - 8):
                                near[s, t, i, pl.ds(half, 8), :] = sides[side, pl.ds(top + half, 8), :]

                for row in range(0, ROWS, SPAN):
                    packed = jnp.zeros((16, 128), jnp.float32)
                    for s, t, i, _, start, y, count in (strip for strip in STRIPS if strip[3] == row):
                        values = pltpu.roll(near[s, t, i], wrapped(start - y - y0), 1)
                        packed = jnp.where((lane >= start) & (lane < start + count), values, packed)
                    spot = n * ROWS + row
                    out[pl.ds(spot, 8), :] = packed[:8]
                    out[pl.ds(spot + 8, SPAN - 8), :] = packed[8:SPAN]

        for out, members in zip(outs, packs):

            def each(n, carry):
                row = jnp.int32(members[0])
                for m, member in enumerate(members[1:], 1):
                    row = jnp.where(n == m, member, row)
                cut(row - 1, out, n)
                return carry

            lax.fori_loop(0, len(members), each, 0)


def pass_kernel(*refs):
    got, outs = refs[: len(FIRST)], refs[len(FIRST) + 1 :]
    row = lax.axis_index("probe")
    for head, rest, source in zip(FIRST, NEXT, got):

        @pl.when(row == head)
        def _():
            for n, out in zip(range(len(rest)), outs):
                out[...] = source[pl.ds((1 + n) * ROWS, ROWS), :]


def march_kernel(width, rows_of, *refs):
    @pl.when(rows_of(lax.axis_index("probe")))
    def _():
        march(width, *refs[:15], *refs[-9:])


def march(
    width, xb, zb, yb, sx, sz, sy, wavelet, wave, stiff, buoy, swap_b, swap_a, swap_c, pstiff, pbuoy, out, prep, fields,
    sides, mid, later, weights, near, sem_out,
):
    first = lax.axis_index("gx") * width
    row = lax.axis_index("probe")
    keep_sides((swap_a, swap_b, swap_c), sides)
    lane = lax.broadcasted_iota(jnp.int32, (DEPTH, 128), 1)
    depth = lax.broadcasted_iota(jnp.int32, (DEPTH, 128), 0)
    top, bottom = depth == 0, depth == DEPTH - 1
    left, right = lane == 0, lane == 127

    def present(s, p):
        if isinstance(p, int) and p < 0:
            return sides[0, plane_rows(3 * s + p + 2), :]
        if isinstance(p, int) and p >= width:
            return sides[1, plane_rows(3 * s + p - width), :]
        return wave[s, 1, plane_rows(p), :]

    def earlier(s, p):
        if isinstance(p, int) and (p < 0 or p >= width):
            return sides[0 if p < 0 else 1, plane_rows(3 * s + 2), :]
        return wave[s, 0, plane_rows(p), :]

    def coefficients(p):
        if isinstance(p, int) and (p < 0 or p >= width):
            side = 0 if p < 0 else 1
            return sides[side, plane_rows(6 + (p + 2 if p < 0 else p - width)), :], sides[side, plane_rows(8), :]
        return buoy[plane_rows(p), :], stiff[plane_rows(p), :]

    def weigh(c, cxm, cxp, czm, czp, k):
        k = 0.5 * k
        edge = k * c
        wide = [k * (c + cxm), k * (c + cxp)]
        total = wide[0] + wide[1]
        for value, outside in (
            (czm, top),
            (czp, bottom),
            (pltpu.roll(c, 1, 1), left),
            (pltpu.roll(c, 127, 1), right),
        ):
            full = k * (c + value)
            total += jnp.where(outside, edge, full)
            wide.append(jnp.where(outside, 0.0, full))
        return wide + [2.0 - total]

    def weighted(w, v, vxm, vxp, vzm, vzp, before):
        near = (w[0] * vxm + w[1] * vxp) + (w[2] * vzm + w[3] * vzp)
        near += w[4] * pltpu.roll(v, 1, 1) + w[5] * pltpu.roll(v, 127, 1)
        return (w[6] * v - before) + near

    def save(w, p):
        for n in range(7):
            weights[n, plane_rows(p), :] = w[n]

    def up(v):
        return pltpu.roll(v, 1, 0)

    def down(v):
        return pltpu.roll(v, DEPTH - 1, 0)

    for p in (-1, 0, width - 1, width):
        c, k = coefficients(p)
        w = weigh(c, coefficients(p - 1)[0], coefficients(p + 1)[0], up(c), down(c), k)
        if 0 <= p < width:
            save(w, p)
        for s in range(2):
            v = present(s, p)
            mid[s, plane_rows(p + 1), :] = weighted(
                w, v, present(s, p - 1), present(s, p + 1), up(v), down(v), earlier(s, p)
            )

    def step_one(p, carry):
        above, below = pl.ds(p * DEPTH - 1, DEPTH), pl.ds(p * DEPTH + 1, DEPTH)
        c, k = coefficients(p)
        w = weigh(c, buoy[plane_rows(p - 1), :], buoy[plane_rows(p + 1), :], buoy[above, :], buoy[below, :], k)
        save(w, p)
        for s in range(2):
            mid[s, plane_rows(p + 1), :] = weighted(
                w, present(s, p), present(s, p - 1), present(s, p + 1), wave[s, 1, above, :], wave[s, 1, below, :],
                earlier(s, p),
            )
        return carry

    lax.fori_loop(1, width - 1, step_one, 0, unroll=width - 2)

    sources = [at(sx, s) - first for s in range(2)]

    def inject(ref, step, low, high, shift):
        for s, x in enumerate(sources):

            @pl.when((row == 0) & (x >= low) & (x < high))
            def _():
                hit = (lane == at(sy, s)) & (depth == at(sz, s))
                spot = plane_rows(x + shift)
                ref[s, spot, :] = ref[s, spot, :] + jnp.where(hit, at(wavelet.at[s], step), 0.0)

    inject(mid, 0, -1, width + 1, 1)
    outs = copy_all([(mid.at[s, plane_rows(1, width)], out.at[s, 0]) for s in range(2)], sem_out)

    def step_two(p, carry):
        above, below = pl.ds((p + 1) * DEPTH - 1, DEPTH), pl.ds((p + 1) * DEPTH + 1, DEPTH)
        w = [weights[n, plane_rows(p), :] for n in range(7)]
        for s in range(2):
            later[s, plane_rows(p), :] = weighted(
                w, mid[s, plane_rows(p + 1), :], mid[s, plane_rows(p), :], mid[s, plane_rows(p + 2), :],
                mid[s, above, :], mid[s, below, :], present(s, p),
            )
        return carry

    part = width // 3
    for n in range(3):
        low, high = n * part, (n + 1) * part
        lax.fori_loop(low, high, step_two, 0, unroll=part)
        inject(later, 1, low, high, 0)
        pairs = [(later.at[s, plane_rows(low, part)], out.at[s, 1, plane_rows(low, part)]) for s in range(2)]
        outs += copy_all(pairs, sem_out, 2 + 2 * n)

    g = jnp.maximum(row - 1, 0)
    x0, z0, y0 = window((xb, zb, yb), g, first)

    @pl.when((row > 0) & met(x0, width))
    def _():
        strip = lax.broadcasted_iota(jnp.int32, (8, 128), 1)
        here = (strip < SPAN) & (strip + y0 >= 0) & (strip + y0 < 128)
        near[...] = jnp.zeros(near.shape, jnp.float32)

        def bring(n, i, load):
            for half in (0, SPAN - 8):
                near[n, i, pl.ds(half, 8), :] = jnp.where(here, pltpu.roll(load(half), wrapped(-y0), 1), 0.0)

        for i in range(SPAN):
            p = x0 + i

            @pl.when((p >= 0) & (p < width))
            def _():
                bring(0, i, lambda half: buoy[pl.ds(p * DEPTH + z0 + half, 8), :])
                bring(1, i, lambda half: stiff[pl.ds(p * DEPTH + z0 + half, 8), :])
                for s in range(2):
                    fields[i, s, 0, pl.ds(0, DEPTH), :] = mid[s, plane_rows(p + 1), :]
                    fields[i, s, 1, pl.ds(0, DEPTH), :] = later[s, plane_rows(p), :]

            side = jnp.where(p < 0, 0, 1)
            j = jnp.where(p < 0, p + 2, p - width)

            @pl.when(((p >= -2) & (p < 0)) | ((p >= width) & (p < width + 2)))
            def _():
                bring(0, i, lambda half: sides[side, pl.ds((6 + j) * DEPTH + z0 + half, 8), :])

            @pl.when((p == -1) | (p == width))
            def _():
                bring(1, i, lambda half: sides[side, pl.ds(8 * DEPTH + z0 + half, 8), :])

        wide = lax.broadcasted_iota(jnp.int32, (EDGE, EDGE, pstiff.shape[-1]), 2)
        diagonal = lax.broadcasted_iota(jnp.int32, (EDGE, EDGE, 128), 2)
        diagonal = diagonal == lax.broadcasted_iota(jnp.int32, (EDGE, EDGE, 128), 1) + 2
        dz = at(zb, g) * EDGE - z0
        for n, ref in ((2, pstiff), (3, pbuoy)):
            for i in range(EDGE):
                column = jnp.sum(jnp.where(wide == g, ref[i], 0.0), axis=2, keepdims=True)
                near[n, 2 + i, pl.ds(dz, EDGE), :] = jnp.sum(jnp.where(diagonal, column, 0.0), axis=1)

        none = jnp.zeros((16, 128), jnp.float32)

        def faces(n, i):
            c = near[n, i]
            x = [0.5 * (c + near[n, i + d]) if 0 <= i + d < SPAN else none for d in (-1, 1)]
            z, y = 0.5 * (c + pltpu.roll(c, 15, 0)), 0.5 * (c + pltpu.roll(c, 127, 1))
            return [*x, pltpu.roll(z, 1, 0), z, pltpu.roll(y, 1, 1), y]

        for i in range(SPAN):
            k, sb = near[1, i], near[2, i]
            forced, free = none, 2.0 + none
            for n, (a, b) in enumerate(zip(faces(0, i), faces(3, i))):
                given, own = sb * a + k * b, k * a
                prep[n, i], prep[7 + n, i] = given, own
                forced, free = forced - given, free - own
            prep[6, i], prep[13, i] = forced, free

    wait_all(outs)


def born_kernel(width, extent, xb, zb, yb, sx, sz, sy, wavelet, *refs):
    count = len(FIRST) + len(DIRECT)
    longest = max(len(rest) for rest in NEXT)
    firsts, directs, nexts = refs[: len(FIRST)], refs[len(FIRST) : count], refs[count : count + longest]
    prep, fields, _, out, piece, planes, now, before, later, forced, sem = refs[count + longest :]
    row = lax.axis_index("probe")
    g = jnp.maximum(row - 1, 0)
    first = lax.axis_index("gx") * width
    x0, z0, y0 = window((xb, zb, yb), g, first)

    @pl.when((row > 0) & met(x0, width))
    def _():
        def bring(where, source):
            @pl.when(where)
            def _():
                piece[pl.ds(0, ROWS), :] = source[pl.ds(0, ROWS), :]

        for target, source in zip(FIRST + DIRECT, (*firsts, *directs)):
            bring(row == target, source)
        for n, source in enumerate(nexts):
            where = row < 0
            for rest in NEXT:
                if n < len(rest):
                    where = where | (row == rest[n])
            bring(where, source)

        planes[...] = fields[...]
        lane = lax.broadcasted_iota(jnp.int32, (16, 128), 1)
        depth = lax.broadcasted_iota(jnp.int32, (16, 128), 0)
        here = (lane < SPAN) & (depth < SPAN) & (lane + y0 >= 0) & (lane + y0 < 128)
        inner = here & (lane >= 1) & (lane < SPAN - 1)
        blank, whole = jnp.zeros((8, 128), jnp.float32), jnp.zeros((GRID, 128), jnp.float32)
        for ref in (now, later, forced):
            for s in range(2):
                for i in range(SPAN + 3):
                    ref[s, pl.ds(i * GRID, 8), :] = blank
                for i in (0, SPAN + 1):
                    ref[s, pl.ds(i * GRID, GRID), :] = whole

        def strip(s, t, i):
            found = [strip for strip in STRIPS if strip[:3] == (s, t, i)]
            if not found:
                return jnp.zeros((16, 128), jnp.float32)
            _, _, _, row, start, y, _ = found[0]
            values = piece[pl.ds(row, 16), :]
            if start != y:
                values = pltpu.roll(values, (y - start) % 128, 1)
            x = x0 + i
            ok = (first + x >= 0) & (first + x < extent) & (x >= -1 - t) & (x < width + 1 + t)
            return jnp.where((here if t else inner) & ok, values, 0.0)

        def cells(i, shift=0):
            start = (i + 1) * GRID
            return pl.ds((start if isinstance(i, int) else pl.multiple_of(start, 8)) + 8 + shift, 16)

        def around(ref, s, i):
            v = ref[s, cells(i), :]
            x = [ref[s, cells(i + d), :] for d in (-1, 1)]
            z = [ref[s, cells(i, d), :] for d in (-1, 1)]
            return [*x, *z, pltpu.roll(v, 1, 1), pltpu.roll(v, 127, 1), v]

        def weighted(w, values):
            a, b, c, d, e, f, g = (x * y for x, y in zip(w, values))
            return ((a + b) + (c + d)) + ((e + f) + g)

        for s in range(2):
            for i in range(SPAN):
                now[s, cells(i), :] = strip(s, 1, i)
                before[s, i] = strip(s, 0, i)
        shots = []
        for s in range(2):
            hit = here & (lane + y0 == at(sy, s)) & (depth + z0 == at(sz, s))
            shots.append((at(sx, s) - first - x0, jnp.where(hit, at(wavelet.at[s], 0), 0.0)))
        def first_pass(i, carry):
            of_forcing, of_step = ([prep[n + m, i] for n in range(7)] for m in (0, 7))
            for s, (x, source) in enumerate(shots):
                values = around(now, s, i)
                forced[s, cells(i), :] = weighted(of_forcing, values)
                after = weighted(of_step, values) - before[s, i]
                later[s, cells(i), :] = after + jnp.where(x == i, source, 0.0)
            return carry

        lax.fori_loop(0, SPAN, first_pass, 0, unroll=3)

        def each_plane(act, low=0, high=SPAN):
            for i in range(low, high):

                @pl.when((x0 + i >= 0) & (x0 + i < width))
                def _():
                    target = out.at[:, :, plane_rows(x0 + i)]
                    act(pltpu.make_async_copy(planes.at[i, :, :, pl.ds(0, DEPTH)], target, sem.at[i]))

        def second_pass(i, carry):
            of_forcing, of_step = ([prep[n + m, i] for n in range(7)] for m in (0, 7))
            for s in range(2):
                gain = forced[s, cells(i), :]
                more = weighted(of_step, around(forced, s, i)) + weighted(of_forcing, around(later, s, i))
                for t, value in enumerate((gain, more)):
                    spot = pl.ds(z0, 16)
                    planes[i, s, t, spot, :] = fields[i, s, t, spot, :] + pltpu.roll(value, wrapped(y0), 1)
            return carry

        part = SPAN // 3
        for low in range(0, SPAN, part):
            lax.fori_loop(low, low + part, second_pass, 0, unroll=2)
            each_plane(lambda copy: copy.start(), low, low + part)
        each_plane(lambda copy: copy.wait())


def on_device(
    wavefields, stiffness, buoyancy, pert_stiffness, pert_buoyancy, xblock_index, zblock_index, yblock_index,
    source_xcell, source_zcell, source_ycell, wavelet
):
    width = wavefields.shape[3]
    slabs = lax.axis_size("gx")
    rows = width * DEPTH
    wave = wavefields.reshape(2, 2, rows, 128)
    stiff, buoy = stiffness.reshape(rows, 128), buoyancy.reshape(rows, 128)
    blocks = (xblock_index, zblock_index, yblock_index)
    sources = (source_xcell, source_zcell, source_ycell, wavelet)
    perts = [jnp.transpose(p, (1, 2, 3, 0)) for p in (pert_stiffness, pert_buoyancy)]
    hbm = lambda *shape: pltpu.HBM(shape, jnp.float32)
    vmem = lambda *shape: pltpu.VMEM(shape, jnp.float32)
    dma = lambda *shape: pltpu.SemaphoreType.DMA(shape)

    def call(kernel, name, out_shape, spaces, scratch, **more):
        made = pl.pallas_call(
            kernel,
            out_shape=out_shape,
            in_specs=[pl.BlockSpec(memory_space=space) for space in spaces],
            out_specs=jax.tree.map(lambda s: pl.BlockSpec(memory_space=s.memory_space), out_shape),
            scratch_shapes=scratch,
            compiler_params=PARAMS,
            name=name,
            **more,
        )
        return lambda *args: made(*map(pltpu.with_memory_space_constraint, args, spaces))

    def along_rows(value, pairs):
        every = [(a * slabs + s, b * slabs + s) for a, b in pairs for s in range(slabs)]
        return lax.ppermute(value, ("probe", "gx"), every)

    def swap(value, pairs):
        both = [(row, a, b) for row, low in pairs for a, b in ((low, low + 1), (low + 1, low))]
        return lax.ppermute(value, ("probe", "gx"), [(row * slabs + a, row * slabs + b) for row, a, b in both])

    edge = vmem(3, 3, DEPTH, 128)
    edge_a, edge_b, edge_c = call(
        functools.partial(edge_kernel, width), "edges", [edge] * 3, [pltpu.HBM] * 3, [dma(8)]
    )(wavefields[0], stiffness, buoyancy)
    edge_a, edge_b, edge_c = (edges.reshape(-1, 128) for edges in (edge_a, edge_b, edge_c))
    rounds = swap_pairs(lax.axis_size("probe"), slabs)
    swaps = [swap(*each) for each in zip((edge_a, edge_b, edge_c), rounds)]

    counts = [1 + len(rest) for rest in NEXT] + [1] * len(DIRECT)
    packs = call(
        functools.partial(split_kernel, width),
        "split",
        [vmem(n * ROWS, 128) for n in counts],
        [pltpu.VMEM] * 7,
        [vmem(2, 9 * DEPTH, 128), vmem(2, 2, SPAN, 16, 128)],
    )(*blocks, wave, swaps[1], swaps[0], swaps[2])
    got = [along_rows(p, [(0, row)]) for p, row in zip(packs, FIRST + DIRECT)]

    def march_on(name, rows_of, before=()):
        marched = [hbm(2, 2, rows, 128), vmem(14, SPAN, 16, 128), vmem(SPAN, 2, 2, DEPTH + 8, 128)]
        operands = (*blocks, *sources, wave, stiff, buoy, swaps[1], swaps[0], swaps[2], *perts, *before)
        return call(
            functools.partial(march_kernel, width, rows_of),
            name,
            marched,
            [pltpu.VMEM] * 15 + [pltpu.HBM, pltpu.VMEM, pltpu.VMEM, pltpu.VMEM][: len(before)],
            [
                vmem(2, 9 * DEPTH, 128),
                vmem(2, (width + 2) * DEPTH, 128),
                vmem(2, rows, 128),
                vmem(7, rows, 128),
                vmem(4, SPAN, 16, 128),
                dma(8),
            ],
            input_output_aliases={15: 0, 16: 1, 17: 2} if before else {},
        )(*operands)

    late = lambda row: functools.reduce(jnp.logical_or, [row == r for r in FIRST])
    marched = march_on("march_first", late)

    longest = max(len(rest) for rest in NEXT)
    passed = call(
        pass_kernel, "pass_on", [vmem(ROWS, 128)] * longest, [pltpu.VMEM] * (len(FIRST) + 1), []
    )(*got[: len(FIRST)], marched[1])
    nexts = [
        along_rows(value, [(head, rest[n]) for head, rest in zip(FIRST, NEXT) if n < len(rest)])
        for n, value in enumerate(passed)
    ]
    advanced, prep, fields = march_on("march_rest", lambda row: jnp.logical_not(late(row)), (*marched, passed[-1]))
    operands = (*blocks, *sources, *got, *nexts, prep, fields, advanced)
    result = call(
        functools.partial(born_kernel, width, width * slabs),
        "born",
        hbm(2, 2, rows, 128),
        [pltpu.VMEM] * (len(operands) - 1) + [pltpu.HBM],
        [
            vmem(ROWS + 8, 128),
            vmem(SPAN, 2, 2, DEPTH + 8, 128),
            vmem(2, (SPAN + 2) * GRID + 8, 128),
            vmem(2, SPAN, 16, 128),
            *[vmem(2, (SPAN + 2) * GRID + 8, 128)] * 2,
            dma(SPAN),
        ],
        input_output_aliases={len(operands) - 1: 0},
    )(*operands)
    return result.reshape(wavefields.shape)


def solution(mesh):
    field = P("probe", None, None, "gx", None, None)
    return jax.shard_map(
        on_device,
        mesh=mesh,
        in_specs=(field, P("gx", None, None), P("gx", None, None)) + (P(),) * 9,
        out_specs=field,
        check_vma=False,
    )
```

```python
import functools

import jax
import jax.numpy as jnp
from jax import lax
from jax.experimental import pallas as pl
from jax.experimental.pallas import tpu as pltpu
from jax.sharding import PartitionSpec as P

EDGE = 8
SPAN = EDGE + 4
DEPTH = 32
GRID = 24
ROWS = 4 * SPAN


def strips_of_a_piece():
    found = []
    for n, (s, i) in enumerate((s, i) for s in range(2) for i in range(SPAN)):
        found.append((s, 1, i, n // 10 * SPAN, n % 10 * SPAN, 0, SPAN))
    for n, (s, i) in enumerate((s, i) for s in range(2) for i in range(1, SPAN - 1)):
        row, lane = (2 * SPAN, 48 + 10 * n) if n < 8 else (3 * SPAN, 10 * (n - 8))
        found.append((s, 0, i, row, lane, 1, 10))
    return found


STRIPS = strips_of_a_piece()

FIRST = (1, 2, 6, 8)
NEXT = ((9, 3, 7, 5), (10, 4, 12), (14, 15), (11,))
DIRECT = (13,)

PARAMS = pltpu.CompilerParams(vmem_limit_bytes=32 * 1024 * 1024)


def copy_all(pairs, sems, start=0):
    copies = [pltpu.make_async_copy(a, b, sems.at[start + n]) for n, (a, b) in enumerate(pairs)]
    for copy in copies:
        copy.start()
    return copies


def wait_all(copies):
    for copy in copies:
        copy.wait()


def wrapped(shift):
    return jnp.bitwise_and(shift + 128, 127)


def plane_rows(p, count=1):
    start = p * DEPTH
    return pl.ds(start if isinstance(p, int) else pl.multiple_of(start, DEPTH), count * DEPTH)


def at(ref, n):
    values = ref[...].reshape(1, -1)
    lane = lax.broadcasted_iota(jnp.int32, values.shape, 1)
    return jnp.sum(jnp.where(lane == n, values, jnp.zeros_like(values)))


def window(blocks, g, first):
    xb, zb, yb = (at(ref, g) for ref in blocks)
    return xb * EDGE - 2 - first, jnp.clip(zb * EDGE - 2, 0, DEPTH - SPAN), yb * EDGE - 2


def met(x0, width):
    return (x0 < width) & (x0 + SPAN > 0)


def from_sides(swap_a, swap_b, act):
    even = lax.rem(lax.axis_index("gx"), 2) == 0

    @pl.when(even)
    def _():
        act(swap_b, swap_a)

    @pl.when(jnp.logical_not(even))
    def _():
        act(swap_a, swap_b)


def edge_kernel(width, wave, stiff, buoy, swap_a, swap_b, sem):
    def pack(low, high):
        pairs = []
        for out, outer, inner in ((low, 0, 0), (high, width - 1, width - 2)):
            pairs.append((wave.at[:, 1, pl.ds(inner, 2)], out.at[pl.ds(0, 2), pl.ds(0, 2)]))
            pairs.append((wave.at[:, 0, outer], out.at[pl.ds(0, 2), 2]))
            pairs.append((buoy.at[pl.ds(inner, 2)], out.at[2, pl.ds(0, 2)]))
            pairs.append((stiff.at[outer], out.at[2, 2]))
        wait_all(copy_all(pairs, sem))

    from_sides(swap_a, swap_b, pack)


def keep_sides(swap_a, swap_b, sides):
    def act(below, above):
        sides[0] = below[...]
        sides[1] = above[...]

    from_sides(swap_a, swap_b, act)


def split_kernel(width, xb, zb, yb, wave, swap_a, swap_b, *refs):
    *outs, sides, near = refs
    packs = [(head, *rest) for head, rest in zip(FIRST, NEXT)] + [(row,) for row in DIRECT]

    @pl.when(lax.axis_index("probe") == 0)
    def _():
        first = lax.axis_index("gx") * width
        keep_sides(swap_a, swap_b, sides)
        lane = lax.broadcasted_iota(jnp.int32, (16, 128), 1)
        starts = xb[...].reshape(1, -1) * EDGE - 2 - first
        each_bit = jnp.left_shift(1, lax.broadcasted_iota(jnp.int32, starts.shape, 1))
        bits = jnp.sum(jnp.where(met(starts, width), each_bit, 0))

        def cut(g, out, n):
            @pl.when(jnp.bitwise_and(jnp.right_shift(bits, g), 1) == 1)
            def _():
                x0, z0, y0 = window((xb, zb, yb), g, first)
                for i in range(SPAN):
                    p = x0 + i

                    @pl.when((p >= 0) & (p < width))
                    def _():
                        for s, t in ((0, 0), (0, 1), (1, 0), (1, 1)):
                            for half in (0, SPAN - 8):
                                near[s, t, i, pl.ds(half, 8), :] = wave[s, t, pl.ds(p * DEPTH + z0 + half, 8), :]

                    @pl.when(((p >= -2) & (p < 0)) | ((p >= width) & (p < width + 2)))
                    def _():
                        side = jnp.where(p < 0, 0, 1)
                        j = jnp.where(p < 0, p + 2, p - width)
                        for s, t in ((0, 0), (0, 1), (1, 0), (1, 1)):
                            top = (3 * s + (j if t else 2)) * DEPTH + z0
                            for half in (0, SPAN - 8):
                                near[s, t, i, pl.ds(half, 8), :] = sides[side, pl.ds(top + half, 8), :]

                for row in range(0, ROWS, SPAN):
                    packed = jnp.zeros((16, 128), jnp.float32)
                    for s, t, i, _, start, y, count in (strip for strip in STRIPS if strip[3] == row):
                        values = pltpu.roll(near[s, t, i], wrapped(start - y - y0), 1)
                        packed = jnp.where((lane >= start) & (lane < start + count), values, packed)
                    spot = n * ROWS + row
                    out[pl.ds(spot, 8), :] = packed[:8]
                    out[pl.ds(spot + 8, SPAN - 8), :] = packed[8:SPAN]

        for out, members in zip(outs, packs):

            def each(n, carry):
                row = jnp.int32(members[0])
                for m, member in enumerate(members[1:], 1):
                    row = jnp.where(n == m, member, row)
                cut(row - 1, out, n)
                return carry

            lax.fori_loop(0, len(members), each, 0)


def pass_kernel(*refs):
    got, outs = refs[: len(FIRST)], refs[len(FIRST) + 1 :]
    row = lax.axis_index("probe")
    for head, rest, source in zip(FIRST, NEXT, got):

        @pl.when(row == head)
        def _():
            for n, out in zip(range(len(rest)), outs):
                out[...] = source[pl.ds((1 + n) * ROWS, ROWS), :]


def march_kernel(width, rows_of, *refs):
    @pl.when(rows_of(lax.axis_index("probe")))
    def _():
        march(width, *refs[:14], *refs[-9:])


def march(
    width, xb, zb, yb, sx, sz, sy, wavelet, wave, stiff, buoy, swap_a, swap_b, pstiff, pbuoy, out, prep, fields,
    sides, mid, later, weights, near, sem_out,
):
    first = lax.axis_index("gx") * width
    row = lax.axis_index("probe")
    keep_sides(swap_a, swap_b, sides)
    lane = lax.broadcasted_iota(jnp.int32, (DEPTH, 128), 1)
    depth = lax.broadcasted_iota(jnp.int32, (DEPTH, 128), 0)
    top, bottom = depth == 0, depth == DEPTH - 1
    left, right = lane == 0, lane == 127

    def present(s, p):
        if isinstance(p, int) and p < 0:
            return sides[0, plane_rows(3 * s + p + 2), :]
        if isinstance(p, int) and p >= width:
            return sides[1, plane_rows(3 * s + p - width), :]
        return wave[s, 1, plane_rows(p), :]

    def earlier(s, p):
        if isinstance(p, int) and (p < 0 or p >= width):
            return sides[0 if p < 0 else 1, plane_rows(3 * s + 2), :]
        return wave[s, 0, plane_rows(p), :]

    def coefficients(p):
        if isinstance(p, int) and (p < 0 or p >= width):
            side = 0 if p < 0 else 1
            return sides[side, plane_rows(6 + (p + 2 if p < 0 else p - width)), :], sides[side, plane_rows(8), :]
        return buoy[plane_rows(p), :], stiff[plane_rows(p), :]

    def weigh(c, cxm, cxp, czm, czp, k):
        k = 0.5 * k
        edge = k * c
        wide = [k * (c + cxm), k * (c + cxp)]
        total = wide[0] + wide[1]
        for value, outside in (
            (czm, top),
            (czp, bottom),
            (pltpu.roll(c, 1, 1), left),
            (pltpu.roll(c, 127, 1), right),
        ):
            full = k * (c + value)
            total += jnp.where(outside, edge, full)
            wide.append(jnp.where(outside, 0.0, full))
        return wide + [2.0 - total]

    def weighted(w, v, vxm, vxp, vzm, vzp, before):
        near = (w[0] * vxm + w[1] * vxp) + (w[2] * vzm + w[3] * vzp)
        near += w[4] * pltpu.roll(v, 1, 1) + w[5] * pltpu.roll(v, 127, 1)
        return (w[6] * v - before) + near

    def save(w, p):
        for n in range(7):
            weights[n, plane_rows(p), :] = w[n]

    def up(v):
        return pltpu.roll(v, 1, 0)

    def down(v):
        return pltpu.roll(v, DEPTH - 1, 0)

    for p in (-1, 0, width - 1, width):
        c, k = coefficients(p)
        w = weigh(c, coefficients(p - 1)[0], coefficients(p + 1)[0], up(c), down(c), k)
        if 0 <= p < width:
            save(w, p)
        for s in range(2):
            v = present(s, p)
            mid[s, plane_rows(p + 1), :] = weighted(
                w, v, present(s, p - 1), present(s, p + 1), up(v), down(v), earlier(s, p)
            )

    def step_one(p, carry):
        above, below = pl.ds(p * DEPTH - 1, DEPTH), pl.ds(p * DEPTH + 1, DEPTH)
        c, k = coefficients(p)
        w = weigh(c, buoy[plane_rows(p - 1), :], buoy[plane_rows(p + 1), :], buoy[above, :], buoy[below, :], k)
        save(w, p)
        for s in range(2):
            mid[s, plane_rows(p + 1), :] = weighted(
                w, present(s, p), present(s, p - 1), present(s, p + 1), wave[s, 1, above, :], wave[s, 1, below, :],
                earlier(s, p),
            )
        return carry

    lax.fori_loop(1, width - 1, step_one, 0, unroll=width - 2)

    sources = [at(sx, s) - first for s in range(2)]

    def inject(ref, step, low, high, shift):
        for s, x in enumerate(sources):

            @pl.when((row == 0) & (x >= low) & (x < high))
            def _():
                hit = (lane == at(sy, s)) & (depth == at(sz, s))
                spot = plane_rows(x + shift)
                ref[s, spot, :] = ref[s, spot, :] + jnp.where(hit, at(wavelet.at[s], step), 0.0)

    inject(mid, 0, -1, width + 1, 1)
    outs = copy_all([(mid.at[s, plane_rows(1, width)], out.at[s, 0]) for s in range(2)], sem_out)

    def step_two(p, carry):
        above, below = pl.ds((p + 1) * DEPTH - 1, DEPTH), pl.ds((p + 1) * DEPTH + 1, DEPTH)
        w = [weights[n, plane_rows(p), :] for n in range(7)]
        for s in range(2):
            later[s, plane_rows(p), :] = weighted(
                w, mid[s, plane_rows(p + 1), :], mid[s, plane_rows(p), :], mid[s, plane_rows(p + 2), :],
                mid[s, above, :], mid[s, below, :], present(s, p),
            )
        return carry

    part = width // 3
    for n in range(3):
        low, high = n * part, (n + 1) * part
        lax.fori_loop(low, high, step_two, 0, unroll=part)
        inject(later, 1, low, high, 0)
        pairs = [(later.at[s, plane_rows(low, part)], out.at[s, 1, plane_rows(low, part)]) for s in range(2)]
        outs += copy_all(pairs, sem_out, 2 + 2 * n)

    g = jnp.maximum(row - 1, 0)
    x0, z0, y0 = window((xb, zb, yb), g, first)

    @pl.when((row > 0) & met(x0, width))
    def _():
        strip = lax.broadcasted_iota(jnp.int32, (8, 128), 1)
        here = (strip < SPAN) & (strip + y0 >= 0) & (strip + y0 < 128)
        near[...] = jnp.zeros(near.shape, jnp.float32)

        def bring(n, i, load):
            for half in (0, SPAN - 8):
                near[n, i, pl.ds(half, 8), :] = jnp.where(here, pltpu.roll(load(half), wrapped(-y0), 1), 0.0)

        for i in range(SPAN):
            p = x0 + i

            @pl.when((p >= 0) & (p < width))
            def _():
                bring(0, i, lambda half: buoy[pl.ds(p * DEPTH + z0 + half, 8), :])
                bring(1, i, lambda half: stiff[pl.ds(p * DEPTH + z0 + half, 8), :])
                for s in range(2):
                    fields[i, s, 0, pl.ds(0, DEPTH), :] = mid[s, plane_rows(p + 1), :]
                    fields[i, s, 1, pl.ds(0, DEPTH), :] = later[s, plane_rows(p), :]

            side = jnp.where(p < 0, 0, 1)
            j = jnp.where(p < 0, p + 2, p - width)

            @pl.when(((p >= -2) & (p < 0)) | ((p >= width) & (p < width + 2)))
            def _():
                bring(0, i, lambda half: sides[side, pl.ds((6 + j) * DEPTH + z0 + half, 8), :])

            @pl.when((p == -1) | (p == width))
            def _():
                bring(1, i, lambda half: sides[side, pl.ds(8 * DEPTH + z0 + half, 8), :])

        wide = lax.broadcasted_iota(jnp.int32, (EDGE, EDGE, pstiff.shape[-1]), 2)
        diagonal = lax.broadcasted_iota(jnp.int32, (EDGE, EDGE, 128), 2)
        diagonal = diagonal == lax.broadcasted_iota(jnp.int32, (EDGE, EDGE, 128), 1) + 2
        dz = at(zb, g) * EDGE - z0
        for n, ref in ((2, pstiff), (3, pbuoy)):
            for i in range(EDGE):
                column = jnp.sum(jnp.where(wide == g, ref[i], 0.0), axis=2, keepdims=True)
                near[n, 2 + i, pl.ds(dz, EDGE), :] = jnp.sum(jnp.where(diagonal, column, 0.0), axis=1)

        none = jnp.zeros((16, 128), jnp.float32)

        def faces(n, i):
            c = near[n, i]
            x = [0.5 * (c + near[n, i + d]) if 0 <= i + d < SPAN else none for d in (-1, 1)]
            z, y = 0.5 * (c + pltpu.roll(c, 15, 0)), 0.5 * (c + pltpu.roll(c, 127, 1))
            return [*x, pltpu.roll(z, 1, 0), z, pltpu.roll(y, 1, 1), y]

        for i in range(SPAN):
            k, sb = near[1, i], near[2, i]
            forced, free = none, 2.0 + none
            for n, (a, b) in enumerate(zip(faces(0, i), faces(3, i))):
                given, own = sb * a + k * b, k * a
                prep[n, i], prep[7 + n, i] = given, own
                forced, free = forced - given, free - own
            prep[6, i], prep[13, i] = forced, free

    wait_all(outs)


def born_kernel(width, extent, xb, zb, yb, sx, sz, sy, wavelet, *refs):
    count = len(FIRST) + len(DIRECT)
    longest = max(len(rest) for rest in NEXT)
    firsts, directs, nexts = refs[: len(FIRST)], refs[len(FIRST) : count], refs[count : count + longest]
    prep, fields, _, out, piece, planes, now, before, later, forced, sem = refs[count + longest :]
    row = lax.axis_index("probe")
    g = jnp.maximum(row - 1, 0)
    first = lax.axis_index("gx") * width
    x0, z0, y0 = window((xb, zb, yb), g, first)

    @pl.when((row > 0) & met(x0, width))
    def _():
        def bring(where, source):
            @pl.when(where)
            def _():
                piece[pl.ds(0, ROWS), :] = source[pl.ds(0, ROWS), :]

        for target, source in zip(FIRST + DIRECT, (*firsts, *directs)):
            bring(row == target, source)
        for n, source in enumerate(nexts):
            where = row < 0
            for rest in NEXT:
                if n < len(rest):
                    where = where | (row == rest[n])
            bring(where, source)

        planes[...] = fields[...]
        lane = lax.broadcasted_iota(jnp.int32, (16, 128), 1)
        depth = lax.broadcasted_iota(jnp.int32, (16, 128), 0)
        here = (lane < SPAN) & (depth < SPAN) & (lane + y0 >= 0) & (lane + y0 < 128)
        inner = here & (lane >= 1) & (lane < SPAN - 1)
        blank, whole = jnp.zeros((8, 128), jnp.float32), jnp.zeros((GRID, 128), jnp.float32)
        for ref in (now, later, forced):
            for s in range(2):
                for i in range(SPAN + 3):
                    ref[s, pl.ds(i * GRID, 8), :] = blank
                for i in (0, SPAN + 1):
                    ref[s, pl.ds(i * GRID, GRID), :] = whole

        def strip(s, t, i):
            found = [strip for strip in STRIPS if strip[:3] == (s, t, i)]
            if not found:
                return jnp.zeros((16, 128), jnp.float32)
            _, _, _, row, start, y, _ = found[0]
            values = piece[pl.ds(row, 16), :]
            if start != y:
                values = pltpu.roll(values, (y - start) % 128, 1)
            x = x0 + i
            ok = (first + x >= 0) & (first + x < extent) & (x >= -1 - t) & (x < width + 1 + t)
            return jnp.where((here if t else inner) & ok, values, 0.0)

        def cells(i, shift=0):
            start = (i + 1) * GRID
            return pl.ds((start if isinstance(i, int) else pl.multiple_of(start, 8)) + 8 + shift, 16)

        def around(ref, s, i):
            v = ref[s, cells(i), :]
            x = [ref[s, cells(i + d), :] for d in (-1, 1)]
            z = [ref[s, cells(i, d), :] for d in (-1, 1)]
            return [*x, *z, pltpu.roll(v, 1, 1), pltpu.roll(v, 127, 1), v]

        def weighted(w, values):
            a, b, c, d, e, f, g = (x * y for x, y in zip(w, values))
            return ((a + b) + (c + d)) + ((e + f) + g)

        for s in range(2):
            for i in range(SPAN):
                now[s, cells(i), :] = strip(s, 1, i)
                before[s, i] = strip(s, 0, i)
        shots = []
        for s in range(2):
            hit = here & (lane + y0 == at(sy, s)) & (depth + z0 == at(sz, s))
            shots.append((at(sx, s) - first - x0, jnp.where(hit, at(wavelet.at[s], 0), 0.0)))
        def first_pass(i, carry):
            of_forcing, of_step = ([prep[n + m, i] for n in range(7)] for m in (0, 7))
            for s, (x, source) in enumerate(shots):
                values = around(now, s, i)
                forced[s, cells(i), :] = weighted(of_forcing, values)
                after = weighted(of_step, values) - before[s, i]
                later[s, cells(i), :] = after + jnp.where(x == i, source, 0.0)
            return carry

        lax.fori_loop(0, SPAN, first_pass, 0, unroll=3)

        def each_plane(act, low=0, high=SPAN):
            for i in range(low, high):

                @pl.when((x0 + i >= 0) & (x0 + i < width))
                def _():
                    target = out.at[:, :, plane_rows(x0 + i)]
                    act(pltpu.make_async_copy(planes.at[i, :, :, pl.ds(0, DEPTH)], target, sem.at[i]))

        def second_pass(i, carry):
            of_forcing, of_step = ([prep[n + m, i] for n in range(7)] for m in (0, 7))
            for s in range(2):
                gain = forced[s, cells(i), :]
                more = weighted(of_step, around(forced, s, i)) + weighted(of_forcing, around(later, s, i))
                for t, value in enumerate((gain, more)):
                    spot = pl.ds(z0, 16)
                    planes[i, s, t, spot, :] = fields[i, s, t, spot, :] + pltpu.roll(value, wrapped(y0), 1)
            return carry

        part = SPAN // 3
        for low in range(0, SPAN, part):
            lax.fori_loop(low, low + part, second_pass, 0, unroll=2)
            each_plane(lambda copy: copy.start(), low, low + part)
        each_plane(lambda copy: copy.wait())


def on_device(
    wavefields, stiffness, buoyancy, pert_stiffness, pert_buoyancy, xblock_index, zblock_index, yblock_index,
    source_xcell, source_zcell, source_ycell, wavelet
):
    width = wavefields.shape[3]
    slabs = lax.axis_size("gx")
    rows = width * DEPTH
    wave = wavefields.reshape(2, 2, rows, 128)
    stiff, buoy = stiffness.reshape(rows, 128), buoyancy.reshape(rows, 128)
    blocks = (xblock_index, zblock_index, yblock_index)
    sources = (source_xcell, source_zcell, source_ycell, wavelet)
    perts = [jnp.transpose(p, (1, 2, 3, 0)) for p in (pert_stiffness, pert_buoyancy)]
    hbm = lambda *shape: pltpu.HBM(shape, jnp.float32)
    vmem = lambda *shape: pltpu.VMEM(shape, jnp.float32)
    dma = lambda *shape: pltpu.SemaphoreType.DMA(shape)

    def call(kernel, name, out_shape, spaces, scratch, **more):
        made = pl.pallas_call(
            kernel,
            out_shape=out_shape,
            in_specs=[pl.BlockSpec(memory_space=space) for space in spaces],
            out_specs=jax.tree.map(lambda s: pl.BlockSpec(memory_space=s.memory_space), out_shape),
            scratch_shapes=scratch,
            compiler_params=PARAMS,
            name=name,
            **more,
        )
        return lambda *args: made(*map(pltpu.with_memory_space_constraint, args, spaces))

    def along_rows(value, pairs):
        every = [(a * slabs + s, b * slabs + s) for a, b in pairs for s in range(slabs)]
        return lax.ppermute(value, ("probe", "gx"), every)

    def swap(value, start):
        pairs = [(a, a + 1) for a in range(start, slabs - 1, 2)]
        return lax.ppermute(value, "gx", pairs + [(b, a) for a, b in pairs])

    edge = vmem(3, 3, DEPTH, 128)
    edge_a, edge_b = call(
        functools.partial(edge_kernel, width), "edges", [edge] * 2, [pltpu.HBM] * 3, [dma(8)]
    )(wavefields[0], stiffness, buoyancy)
    swap_a, swap_b = swap(edge_a.reshape(-1, 128), 0), swap(edge_b.reshape(-1, 128), 1)

    counts = [1 + len(rest) for rest in NEXT] + [1] * len(DIRECT)
    packs = call(
        functools.partial(split_kernel, width),
        "split",
        [vmem(n * ROWS, 128) for n in counts],
        [pltpu.VMEM] * 6,
        [vmem(2, 9 * DEPTH, 128), vmem(2, 2, SPAN, 16, 128)],
    )(*blocks, wave, swap_a, swap_b)
    got = [along_rows(p, [(0, row)]) for p, row in zip(packs, FIRST + DIRECT)]

    def march_on(name, rows_of, before=()):
        marched = [hbm(2, 2, rows, 128), vmem(14, SPAN, 16, 128), vmem(SPAN, 2, 2, DEPTH + 8, 128)]
        operands = (*blocks, *sources, wave, stiff, buoy, swap_a, swap_b, *perts, *before)
        return call(
            functools.partial(march_kernel, width, rows_of),
            name,
            marched,
            [pltpu.VMEM] * 14 + [pltpu.HBM, pltpu.VMEM, pltpu.VMEM, pltpu.VMEM][: len(before)],
            [
                vmem(2, 9 * DEPTH, 128),
                vmem(2, (width + 2) * DEPTH, 128),
                vmem(2, rows, 128),
                vmem(7, rows, 128),
                vmem(4, SPAN, 16, 128),
                dma(8),
            ],
            input_output_aliases={14: 0, 15: 1, 16: 2} if before else {},
        )(*operands)

    late = lambda row: functools.reduce(jnp.logical_or, [row == r for r in FIRST])
    marched = march_on("march_first", late)

    longest = max(len(rest) for rest in NEXT)
    passed = call(
        pass_kernel, "pass_on", [vmem(ROWS, 128)] * longest, [pltpu.VMEM] * (len(FIRST) + 1), []
    )(*got[: len(FIRST)], marched[1])
    nexts = [
        along_rows(value, [(head, rest[n]) for head, rest in zip(FIRST, NEXT) if n < len(rest)])
        for n, value in enumerate(passed)
    ]
    advanced, prep, fields = march_on("march_rest", lambda row: jnp.logical_not(late(row)), (*marched, passed[-1]))
    operands = (*blocks, *sources, *got, *nexts, prep, fields, advanced)
    result = call(
        functools.partial(born_kernel, width, width * slabs),
        "born",
        hbm(2, 2, rows, 128),
        [pltpu.VMEM] * (len(operands) - 1) + [pltpu.HBM],
        [
            vmem(ROWS + 8, 128),
            vmem(SPAN, 2, 2, DEPTH + 8, 128),
            vmem(2, (SPAN + 2) * GRID + 8, 128),
            vmem(2, SPAN, 16, 128),
            *[vmem(2, (SPAN + 2) * GRID + 8, 128)] * 2,
            dma(SPAN),
        ],
        input_output_aliases={len(operands) - 1: 0},
    )(*operands)
    return result.reshape(wavefields.shape)


def solution(mesh):
    field = P("probe", None, None, "gx", None, None)
    return jax.shard_map(
        on_device,
        mesh=mesh,
        in_specs=(field, P("gx", None, None), P("gx", None, None)) + (P(),) * 9,
        out_specs=field,
        check_vma=False,
    )
```
